128 devices in a mesh: wide: 64 (over y, z, x_lo, core), narrow: 2 (over x_hi).
Axes of the slice: x: 4 (x_hi: 2, x_lo: 2; x = x_hi * 2 + x_lo), y: 4, z: 4, core: 2. Of those that a mesh axis runs over, the one named last changes fastest.
Arguments:
- moments: float32 [8192, 1024], P(('wide', 'narrow')), may hold values from -6 to 6
- up_0: bfloat16 [8192, 4096], P(('wide', 'narrow')), may hold values from -0.5 to 0.5
- up_1: bfloat16 [2048, 4096], P(('wide', 'narrow')), may hold values from -0.5 to 0.5
- up_2: bfloat16 [512, 4096], P(('wide', 'narrow')), may hold values from -0.5 to 0.5
- up_3: bfloat16 [128, 4096], P(('wide', 'narrow')), may hold values from -0.5 to 0.5
- couple_0: bfloat16 [229376, 4096], P(('wide', 'narrow')), may hold values from -0.125 to 0.125
- couple_1: bfloat16 [57344, 4096], P(('wide', 'narrow')), may hold values from -0.125 to 0.125
- couple_2: bfloat16 [14336, 4096], P(('wide', 'narrow')), may hold values from -0.125 to 0.125
- couple_3: bfloat16 [3584, 4096], P(('wide', 'narrow')), may hold values from -0.125 to 0.125
- couple_4: bfloat16 [896, 4096], P(('wide', 'narrow')), may hold values from -0.125 to 0.125
- sources_0: int32 [229376], P(('wide', 'narrow')), may hold values from 0 to 8191, as said below
- sources_1: int32 [57344], P(('wide', 'narrow')), may hold values from 0 to 2047, as said below
- sources_2: int32 [14336], P(('wide', 'narrow')), may hold values from 0 to 511, as said below
- sources_3: int32 [3584], P(('wide', 'narrow')), may hold values from 0 to 127, as said below
- sources_4: int32 [896], P(('wide', 'narrow')), may hold values from 0 to 31, as said below
- counts_0: int32 [8192], P(('wide', 'narrow')), may hold values from 14 to 28, as said below
- counts_1: int32 [2048], P(('wide', 'narrow')), may hold values from 14 to 28, as said below
- counts_2: int32 [512], P(('wide', 'narrow')), may hold values from 14 to 28, as said below
- counts_3: int32 [128], P(('wide', 'narrow')), may hold values from 14 to 28, as said below
- counts_4: int32 [32], replicated, may hold values from 14 to 28, as said below
Outputs:
- far_local: float32 [8192, 1024], P(('wide', 'narrow'))
The draws below stay inside these ranges and needn't reach their ends.
Inputs may be any that keep to these rules, and one draw needn't show every extreme that they name: `sources_0`: slot s belongs to box floor(s / 28). With the level's boxes split evenly over all devices in tree order, every source lies in a box of a device at most 4 devices away from the device of the slot's box; that distance 4 is reached on both sides. `sources_1`: as for sources_0, at level 1. `sources_2`: as for sources_0, at level 2. `sources_3`: as for sources_0, at level 3. `sources_4`: slot s belongs to box floor(s / 28); sources may be any box of level 4. Only the first counts_0[t] slots of box t are valid. Only the first counts_1[t] slots of box t are valid. Only the first counts_2[t] slots of box t are valid. Only the first counts_3[t] slots of box t are valid. Only the first counts_4[t] slots of box t are valid.
All inputs are finite; a program needn't handle non-finite values.
Results may differ from the reference program's by a relative error of at most 0.014.
Values may be sent and summed in bfloat16 or wider, within the bound.
A program may use at most 192 MiB of HBM per device.

```python
import jax
import jax.numpy as jnp
from jax import lax

RANK = 64
RHS = 16
LIST = 28
BOX_DEV = 64
REACH = 4
NBOX_0 = 8192
NBOX_1 = 2048
NBOX_2 = 512
NBOX_3 = 128
NBOX_4 = 32


def list_draw(seed_key, level_index, boxes):
    slot_total = boxes * LIST
    slot_index = jnp.arange(slot_total, dtype=jnp.int32)
    per_device = BOX_DEV // 4 ** level_index
    devices = NBOX_0 // BOX_DEV
    target = slot_index // LIST
    within = slot_index % LIST
    owner = target // per_device
    first_key, second_key = jax.random.split(seed_key)
    offset = jax.random.randint(first_key, (slot_total,), -REACH, REACH + 1)
    leading = target % per_device == 0
    lowest = leading & (within == 0)
    highest = leading & (within == 1)
    offset = jnp.where(lowest, -REACH, jnp.where(highest, REACH, offset))
    device = jnp.clip(owner + offset, 0, devices - 1)
    inner = jax.random.randint(second_key, (slot_total,), 0, per_device)
    inner = jnp.where(lowest, 0, jnp.where(highest, per_device - 1, inner))
    return (device * per_device + inner).astype(jnp.int32)


def count_draw(seed_key, boxes):
    values = jax.random.randint(seed_key, (boxes,), LIST // 2, LIST + 1)
    values = values.at[0].set(LIST).at[1].set(LIST // 2)
    return values.astype(jnp.int32)


def draw_sources_0(key, part):
    key = jax.random.fold_in(key, 11)
    return list_draw(key, 0, NBOX_0)


def draw_sources_1(key, part):
    key = jax.random.fold_in(key, 12)
    return list_draw(key, 1, NBOX_1)


def draw_sources_2(key, part):
    key = jax.random.fold_in(key, 13)
    return list_draw(key, 2, NBOX_2)


def draw_sources_3(key, part):
    key = jax.random.fold_in(key, 14)
    return list_draw(key, 3, NBOX_3)


def draw_sources_4(key, part):
    key = jax.random.fold_in(key, 15)
    slot_total = NBOX_4 * LIST
    values = jax.random.randint(key, (slot_total,), 0, NBOX_4)
    values = values.at[0].set(0).at[1].set(NBOX_4 - 1)
    return values.astype(jnp.int32)


def draw_counts_0(key, part):
    key = jax.random.fold_in(key, 21)
    return count_draw(key, NBOX_0)


def draw_counts_1(key, part):
    key = jax.random.fold_in(key, 22)
    return count_draw(key, NBOX_1)


def draw_counts_2(key, part):
    key = jax.random.fold_in(key, 23)
    return count_draw(key, NBOX_2)


def draw_counts_3(key, part):
    key = jax.random.fold_in(key, 24)
    return count_draw(key, NBOX_3)


def draw_counts_4(key, part):
    key = jax.random.fold_in(key, 25)
    return count_draw(key, NBOX_4)


def block_scale(rng, shape, cuts, least, top_value):
    def one(dim, parts):
        draws = jax.random.uniform(jax.random.fold_in(jax.random.fold_in(rng, 6), dim), (parts,), jnp.float32, least / len(cuts), top_value / len(cuts))
        return jnp.repeat(jnp.exp(draws), shape[dim] // parts).reshape((-1,) + (1,) * (len(shape) - dim - 1))

    level = one(*cuts[0])
    for cut in cuts[1:]:
        level = level * one(*cut)
    return level


def normal_values(key, shape, width, limit, cuts=(), held_as=jnp.bfloat16):
    drawn = width * jax.random.normal(key, shape, jnp.float32)
    if cuts:
        drawn = drawn * block_scale(key, shape, cuts, -0.22, 0.18)
    return jnp.clip(drawn, -limit, limit).astype(held_as)


def setup_inputs(seed: int = 0) -> dict:
    arg_keys = jax.random.split(jax.random.key(seed), 21)
    return {
        "moments": normal_values(arg_keys[0], (NBOX_0, RHS * RANK), 1.0, 6.0, ((0, 128),), jnp.float32),
        "up_0": normal_values(arg_keys[1], (NBOX_0, RANK * RANK), (2 * RANK) ** -0.5, 0.5, ((0, 128),)),
        "up_1": normal_values(arg_keys[2], (NBOX_1, RANK * RANK), (2 * RANK) ** -0.5, 0.5, ((0, 128),)),
        "up_2": normal_values(arg_keys[3], (NBOX_2, RANK * RANK), (2 * RANK) ** -0.5, 0.5, ((0, 128),)),
        "up_3": normal_values(arg_keys[4], (NBOX_3, RANK * RANK), (2 * RANK) ** -0.5, 0.5, ((0, 128),)),
        "couple_0": normal_values(arg_keys[5], (NBOX_0 * LIST, RANK * RANK), (LIST * RANK) ** -0.5, 0.125, ((0, 128),)),
        "couple_1": normal_values(arg_keys[6], (NBOX_1 * LIST, RANK * RANK), (LIST * RANK) ** -0.5, 0.125, ((0, 128),)),
        "couple_2": normal_values(arg_keys[7], (NBOX_2 * LIST, RANK * RANK), (LIST * RANK) ** -0.5, 0.125, ((0, 128),)),
        "couple_3": normal_values(arg_keys[8], (NBOX_3 * LIST, RANK * RANK), (LIST * RANK) ** -0.5, 0.125, ((0, 128),)),
        "couple_4": normal_values(arg_keys[9], (NBOX_4 * LIST, RANK * RANK), (LIST * RANK) ** -0.5, 0.125, ((0, 128),)),
        "sources_0": draw_sources_0(jax.random.fold_in(arg_keys[20], 71), 0),
        "sources_1": draw_sources_1(jax.random.fold_in(arg_keys[20], 71), 0),
        "sources_2": draw_sources_2(jax.random.fold_in(arg_keys[20], 71), 0),
        "sources_3": draw_sources_3(jax.random.fold_in(arg_keys[20], 71), 0),
        "sources_4": draw_sources_4(jax.random.fold_in(arg_keys[20], 71), 0),
        "counts_0": draw_counts_0(jax.random.fold_in(arg_keys[20], 71), 0),
        "counts_1": draw_counts_1(jax.random.fold_in(arg_keys[20], 71), 0),
        "counts_2": draw_counts_2(jax.random.fold_in(arg_keys[20], 71), 0),
        "counts_3": draw_counts_3(jax.random.fold_in(arg_keys[20], 71), 0),
        "counts_4": draw_counts_4(jax.random.fold_in(arg_keys[20], 71), 0),
    }


def lift_level(moment_rows, transfer):
    boxes = moment_rows.shape[0]
    product = jnp.einsum('crk,ckq->crq', moment_rows.reshape(boxes, RHS, RANK).astype(jnp.float32),
                         transfer.reshape(boxes, RANK, RANK).astype(jnp.float32))
    return product.reshape(boxes // 4, 4, RHS * RANK).sum(axis=1)


def lower_level(far_rows, parent_field, transfer):
    boxes = transfer.shape[0]
    parent_rows = jnp.repeat(parent_field.astype(jnp.bfloat16), 4, axis=0)
    product = jnp.einsum('crq,ckq->crk', parent_rows.reshape(boxes, RHS, RANK).astype(jnp.float32),
                         transfer.reshape(boxes, RANK, RANK).astype(jnp.float32))
    return far_rows + product.reshape(boxes, RHS * RANK)


def far_field(moment_rows, couple, sources, counts):
    boxes = counts.shape[0]
    block_size = min(boxes, 256)
    block_count = boxes // block_size
    blocks = couple.reshape(block_count, block_size, LIST, RANK, RANK)
    source_rows = sources.reshape(block_count, block_size, LIST)
    limits = counts.reshape(block_count, block_size)

    def one_block(packed):
        block_coupling, block_sources, block_limits = packed
        picked = moment_rows[block_sources]
        valid = jnp.arange(LIST, dtype=jnp.int32)[None, :] < block_limits[:, None]
        picked = jnp.where(valid[:, :, None], picked, jnp.zeros_like(picked))
        picked = picked.reshape(block_size, LIST, RHS, RANK).astype(jnp.float32)
        result = jnp.einsum('tjrk,tjkq->trq', picked, block_coupling.astype(jnp.float32))
        return result.reshape(block_size, RHS * RANK)

    return lax.map(one_block, (blocks, source_rows, limits)).reshape(boxes, RHS * RANK)


def reference(moments, up_0, up_1, up_2, up_3, couple_0, couple_1, couple_2, couple_3, couple_4,
              sources_0, sources_1, sources_2, sources_3, sources_4,
              counts_0, counts_1, counts_2, counts_3, counts_4):
    transfers = [up_0, up_1, up_2, up_3]
    couplings = [couple_0, couple_1, couple_2, couple_3, couple_4]
    source_lists = [sources_0, sources_1, sources_2, sources_3, sources_4]
    count_lists = [counts_0, counts_1, counts_2, counts_3, counts_4]
    rounded = [moments.astype(jnp.bfloat16)]
    for level_index in range(4):
        moment_next = lift_level(rounded[level_index], transfers[level_index])
        rounded.append(moment_next.astype(jnp.bfloat16))
    far_terms = [far_field(rounded[level_index], couplings[level_index], source_lists[level_index],
                           count_lists[level_index]) for level_index in range(5)]
    field_rows = far_terms[4]
    for level_index in (3, 2, 1, 0):
        field_rows = lower_level(far_terms[level_index], field_rows, transfers[level_index])
    return field_rows
```

```python
import functools

import jax
import jax.numpy as jnp
from jax import lax
from jax.experimental import pallas as pl
from jax.experimental.pallas import tpu as pltpu
from jax.sharding import PartitionSpec as P

RANK = 64
RHS = 16
LIST = 28
REACH = 4
WIDTH = RHS * RANK
BLOCK = RANK * RANK
LANES = 128
SUPER = 4 * LIST
GROUPS = SUPER // 16
WINDOW = 2 * REACH + 1
MESH = pl.DeviceIdType.MESH
BF16 = jnp.bfloat16
F32 = jnp.float32

TOUCH = [
    [b for b in range(4) if b * LIST < 16 * g + 16 and (b + 1) * LIST > 16 * g]
    for g in range(GROUPS)
]


def low_lanes(shape):
    return lax.broadcasted_iota(jnp.int32, shape, 1) < RANK


def swap_halves(value):
    return pltpu.roll(value, RANK, 1)


def kernel(
    devices,
    moments,
    up_0,
    up_1,
    up_2,
    up_3,
    couple_0,
    couple_1,
    couple_2,
    couple_3,
    couple_4,
    sources_0,
    sources_1,
    sources_2,
    sources_3,
    sources_4,
    counts_0,
    counts_1,
    counts_2,
    counts_3,
    counts_4,
    out,
    mom,
    u0,
    u1,
    u2,
    u3,
    c0,
    c1,
    c2,
    c3,
    c4,
    s0,
    pad3,
    pad4,
    tiles,
    rows_b,
    perm,
    win_a,
    win_b,
    up_f,
    up_b,
    lines,
    index,
    gathered,
    far,
    terms,
    top,
    parts,
    load_sem,
    send_a,
    recv_a,
    send_b,
    recv_b,
    send_t,
    recv_t,
    send_m,
    recv_m,
    send_f,
    recv_f,
):
    tops = devices // 4
    me = lax.axis_index("wide") * 2 + lax.axis_index("narrow")
    member = lax.rem(me, 4)
    group = lax.div(me, 4)

    def place(position):
        return (lax.div(position, 2), lax.rem(position, 2))

    def shifted(by):
        return lax.rem(me + by + devices, devices)

    def mate(v):
        return group * 4 + lax.rem(member + v, 4)

    offsets = [o for o in range(-REACH, REACH + 1) if o != 0]

    barrier = pltpu.get_barrier_semaphore()
    for o in offsets:
        pl.semaphore_signal(barrier, inc=1, device_id=place(shifted(o)), device_id_type=MESH)

    def greet(u, carry):
        pl.semaphore_signal(
            barrier, inc=1, device_id=place(shifted(4 * u)), device_id_type=MESH
        )
        return carry

    lax.fori_loop(2, tops - 1, greet, 0)

    loads = [
        (moments, mom),
        (up_0, u0),
        (up_1, u1),
        (up_2, u2),
        (up_3, u3),
        (sources_0, s0),
        (couple_3, c3),
        (couple_4, c4),
        (couple_0, c0),
        (couple_1, c1),
        (couple_2, c2),
    ]
    copies = [
        pltpu.make_async_copy(src, dst, load_sem.at[n]) for n, (src, dst) in enumerate(loads)
    ]
    for copy in copies:
        copy.start()

    def build_perm(j, carry):
        a = lax.broadcasted_iota(jnp.int32, (LANES, WIDTH), 0)
        b = lax.broadcasted_iota(jnp.int32, (LANES, WIDTH), 1)
        wanted = (a % RANK) * RHS + (a // RANK) * 8 + j
        start = pl.multiple_of(j * LANES, LANES)
        perm[pl.ds(start, LANES), :] = jnp.where(wanted == b, 1.0, 0.0).astype(BF16)
        return carry

    lax.fori_loop(0, 8, build_perm, 0)

    copies[0].wait()
    win_a[REACH] = jnp.dot(
        mom[...].astype(BF16), perm[...], preferred_element_type=F32
    ).astype(BF16)

    pl.semaphore_wait(barrier, len(offsets) + tops - 3)

    def exchange(window, send, recv):
        return [
            pltpu.make_async_remote_copy(
                src_ref=window.at[REACH],
                dst_ref=window.at[REACH - o],
                send_sem=send.at[n],
                recv_sem=recv.at[REACH - o],
                device_id=place(shifted(o)),
                device_id_type=MESH,
            )
            for n, o in enumerate(offsets)
        ]

    sends_a = exchange(win_a, send_a, recv_a)
    for copy in sends_a:
        copy.start()

    for n in range(1, 5):
        copies[n].wait()
    bases = [0, 64, 80, 84]

    def spread(m, carry):
        lane = pl.ds(pl.multiple_of(m * LANES, LANES), LANES)
        for source, base, boxes in ((u0, 0, 64), (u1, 64, 16), (u2, 80, 4), (u3, 84, 1)):
            block = source[:, lane].astype(F32)
            other = swap_halves(block)
            step = min(boxes, 8)
            for first in range(0, boxes, step):
                for kp, value in ((0, block), (1, other)):
                    start = (base + first) * RANK + 2 * m + kp
                    piece = value[first : first + step]
                    if step > 1:
                        up_f[pl.ds(start, step, stride=RANK), :] = piece
                    else:
                        up_f[pl.ds(start, 1), :] = piece
        return carry

    lax.fori_loop(0, 32, spread, 0)

    def narrowed(n, carry):
        rows = pl.ds(pl.multiple_of(n * 320, 320), 320)
        up_b[rows, :] = up_f[rows, :].astype(BF16)
        return carry

    lax.fori_loop(0, 17, narrowed, 0)

    for big in range(8):
        for j in range(8):
            tiles[pl.ds((big * 8 + j) * 8, 8), :] = mom[
                big * 8 : big * 8 + 8, j * LANES : (j + 1) * LANES
            ]

    low = low_lanes((8, LANES))

    def beside(first, second):
        even = jnp.where(low, first, swap_halves(second))
        odd = jnp.where(low, swap_halves(first), second)
        return jnp.concatenate([even, odd], axis=0)

    def lifted(children, base):
        left = beside(children[0], children[1])
        right = beside(children[2], children[3])
        rows = jnp.concatenate([left, right], axis=1).astype(BF16)
        product = jnp.dot(
            rows, up_b[base * RANK : (base + 4) * RANK, :], preferred_element_type=F32
        )
        return jnp.where(low, product[:8], swap_halves(product[8:]))

    def tile_of(box):
        return tiles[pl.ds((box // 8) * 64 + box % 8, 8, stride=8), :]

    level_1 = [lifted([tile_of(4 * p + c) for c in range(4)], 4 * p) for p in range(16)]
    level_2 = [lifted(level_1[4 * p : 4 * p + 4], 64 + 4 * p) for p in range(4)]
    level_3 = lifted(level_2, 80)
    alone = jnp.concatenate([level_3, swap_halves(level_3)], axis=0)[:, :RANK].astype(BF16)
    product = jnp.dot(alone, up_b[84 * RANK : 85 * RANK, :], preferred_element_type=F32)
    terms[0] = jnp.where(low, product[:8], swap_halves(product[8:]))

    def to_mates(buffer, send, recv):
        return [
            pltpu.make_async_remote_copy(
                src_ref=buffer.at[0],
                dst_ref=buffer.at[4 - v],
                send_sem=send.at[v],
                recv_sem=recv.at[4 - v],
                device_id=place(mate(v)),
                device_id_type=MESH,
            )
            for v in (1, 2, 3)
        ]

    sends_t = to_mates(terms, send_t, recv_t)
    for copy in sends_t:
        copy.start()

    rows_b[...] = jnp.zeros_like(rows_b)
    for row, value in enumerate(level_1 + level_2 + [level_3]):
        rows_b[pl.ds((row // 8) * 64 + row % 8, 8, stride=8), :] = value
    natural = jnp.concatenate(
        [
            jnp.concatenate(
                [rows_b[(big * 8 + j) * 8 : (big * 8 + j) * 8 + 8, :] for j in range(8)], axis=1
            )
            for big in range(4)
        ],
        axis=0,
    ).astype(BF16)
    win_b[REACH] = jnp.dot(natural, perm[...], preferred_element_type=F32).astype(BF16)
    sends_b = exchange(win_b, send_b, recv_b)
    for copy in sends_b:
        copy.start()

    copies[5].wait()
    first = me - REACH
    for j in range(14):
        lines[j : j + 1, :] = s0[pl.ds(j * LANES, LANES)].reshape(1, LANES) - first * 64
    lines[14:32, :] = jnp.zeros((18, LANES), jnp.int32)
    for j in range(4):
        length = min(LANES, 448 - j * LANES)
        local = sources_1[pl.ds(j * LANES, length)].reshape(1, length) - first * 16
        lines[14 + j : 15 + j, :length] = (local >> 4) * 32 + (local & 15)
    local = sources_2[...].reshape(1, 112) - first * 4
    lines[18:19, :112] = (local >> 2) * 32 + 16 + (local & 3)
    lines[19:20, :28] = (sources_3[...].reshape(1, 28) - first) * 32 + 20
    lines[20:21, :7] = (sources_4[...].reshape(1, 7) - group) & (tops - 1)
    columns = lines[...].T
    for j in range(21):
        index[j * LANES : (j + 1) * LANES, :] = jnp.broadcast_to(
            columns[:, j : j + 1], (LANES, LANES)
        )

    slot = lax.broadcasted_iota(jnp.int32, (SUPER, LANES), 0)

    def drop_invalid(base, counts):
        limit = counts[3] + 3 * LIST
        for b in (2, 1, 0):
            limit = jnp.where(slot < (b + 1) * LIST, counts[b] + b * LIST, limit)
        rows = pl.ds(base, SUPER)
        index[rows, :] = jnp.where(slot < limit, index[rows, :], -1)

    def drop_level(first_row, counts_ref, n):
        def step(n, carry):
            base = pl.multiple_of(first_row + n * SUPER, 16)
            drop_invalid(base, [counts_ref[4 * n + b] for b in range(4)])
            return carry

        lax.fori_loop(0, n, step, 0)

    drop_level(0, counts_0, 16)
    drop_level(1792, counts_1, 4)
    drop_level(2304, counts_2, 1)
    few = lax.broadcasted_iota(jnp.int32, (32, LANES), 0)
    index[2432:2464, :] = jnp.where(few < counts_3[0], index[2432:2464, :], -1)
    left = jnp.minimum(counts_4[group] - member * 7, 7)
    index[2560:2592, :] = jnp.where(few < left, index[2560:2592, :], -1)

    for copy in sends_t:
        copy.wait_recv()
    top[0] = (terms[0] + terms[1]) + (terms[2] + terms[3])

    def to_top(u):
        return pltpu.make_async_remote_copy(
            src_ref=top.at[0],
            dst_ref=top.at[tops - u],
            send_sem=send_m,
            recv_sem=recv_m,
            device_id=place(shifted(4 * u)),
            device_id_type=MESH,
        )

    def send_top(u, carry):
        to_top(u).start()
        return carry

    lax.fori_loop(1, tops, send_top, 0)

    def picked(start, count, sources, width):
        place_of = index[pl.ds(start, count), :]
        lane = lax.broadcasted_iota(jnp.int32, (count, LANES), 1)
        hot = [
            jnp.where(place_of == lane + first_lane, 1.0, 0.0).astype(BF16)[
                :, : min(LANES, width - first_lane)
            ]
            for first_lane in range(0, width, LANES)
        ]
        hot = jnp.concatenate(hot, axis=1) if len(hot) > 1 else hot[0]
        return jnp.dot(hot, sources, preferred_element_type=F32).astype(BF16)

    def gather(start, to, count, window, width):
        for piece in range(0, WIDTH, 256):
            sources = window[:, :, piece : piece + 256].reshape(width, 256)
            gathered[pl.ds(to, count), piece : piece + 256] = picked(
                start, count, sources, width
            )

    def turned(rows):
        stack = jnp.concatenate(
            [rows[:, i * LANES : (i + 1) * LANES] for i in range(8)], axis=0
        )
        across = stack.T
        return jnp.concatenate([across[32 * m : 32 * m + 32] for m in range(4)], axis=1)

    def stacked(rows):
        return jnp.concatenate(
            [
                rows[:, (4 * i + m) * LANES : (4 * i + m + 1) * LANES]
                for m in range(4)
                for i in range(8)
            ],
            axis=0,
        )

    def box_tile(value):
        a, b, c, d = (value[8 * n : 8 * n + 8] for n in range(4))
        return jnp.where(low, a, d) + swap_halves(jnp.where(low, b, c))

    def far_super(rows_from, couple, couple_from, far_from):
        totals = [None] * 4
        lane_slot = lax.broadcasted_iota(jnp.int32, (32, 512), 1) % 16
        for g in range(GROUPS):
            left = turned(gathered[pl.ds(rows_from + 16 * g, 16), :])
            right = stacked(couple[pl.ds(couple_from + 16 * g, 16), :])
            boxes = TOUCH[g]
            if len(boxes) == 2:
                border = boxes[1] * LIST - 16 * g
                zero = jnp.zeros_like(left)
                left = jnp.concatenate(
                    [
                        jnp.where(lane_slot < border, left, zero),
                        jnp.where(lane_slot < border, zero, left),
                    ],
                    axis=0,
                )
            value = jnp.dot(left, right, preferred_element_type=F32)
            for n, b in enumerate(boxes):
                part = value[32 * n : 32 * n + 32]
                totals[b] = part if totals[b] is None else totals[b] + part
        for b in range(4):
            far[pl.ds(far_from + 8 * b, 8), :] = box_tile(totals[b])

    for copy in sends_a:
        copy.wait_recv()

    def gather_0(n, carry):
        start = pl.multiple_of(n * 448, 448)
        gather(start, start, 448, win_a, WINDOW * 64)
        return carry

    lax.fori_loop(0, 4, gather_0, 0)
    copies[8].wait()

    def far_0(n, carry):
        start = pl.multiple_of(n * SUPER, SUPER)
        far_super(start, c0, start, pl.multiple_of(n * 32, 32))
        return carry

    lax.fori_loop(0, 16, far_0, 0)

    copies[6].wait()
    copies[7].wait()
    pad4[...] = jnp.zeros_like(pad4)
    pad4[0:7, :] = c4[...].astype(F32)
    pad3[...] = jnp.zeros_like(pad3)
    pad3[0:28, :] = c3[...].astype(F32)

    def all_top(n):
        return pltpu.make_async_copy(
            top.at[pl.ds(1, tops - 1)], top.at[pl.ds(1, tops - 1)], n
        )

    all_top(recv_m).wait()
    count = max(tops, 8)
    if tops < 8:
        tiles[0:512, :] = jnp.zeros((512, LANES), F32)
    for row in range(tops):
        tiles[pl.ds((row // 8) * 64 + row % 8, 8, stride=8), :] = top[row]
    natural = jnp.concatenate(
        [
            jnp.concatenate(
                [tiles[(big * 8 + j) * 8 : (big * 8 + j) * 8 + 8, :] for j in range(8)], axis=1
            )
            for big in range(count // 8)
        ],
        axis=0,
    ).astype(BF16)
    top_rows = jnp.dot(natural, perm[...], preferred_element_type=F32).astype(BF16)
    left = turned(picked(2560, 16, top_rows, count))
    right = stacked(pad4[...].astype(BF16))
    parts[0] = box_tile(jnp.dot(left, right, preferred_element_type=F32))
    sends_f = to_mates(parts, send_f, recv_f)
    for copy in sends_f:
        copy.start()

    for copy in sends_b:
        copy.wait_recv()
    copies[9].wait()
    copies[10].wait()
    gather(1792, 0, 448, win_b, WINDOW * 32)
    gather(2304, 448, SUPER, win_b, WINDOW * 32)
    gather(2432, 560, 32, win_b, WINDOW * 32)

    def far_1(n, carry):
        start = pl.multiple_of(n * SUPER, SUPER)
        far_super(start, c1, start, pl.multiple_of(512 + n * 32, 32))
        return carry

    lax.fori_loop(0, 4, far_1, 0)
    far_super(448, c2, 0, 640)
    total = None
    for g in range(2):
        left = turned(gathered[560 + 16 * g : 576 + 16 * g, :])
        right = stacked(pad3[16 * g : 16 * g + 16, :].astype(BF16))
        value = jnp.dot(left, right, preferred_element_type=F32)
        total = value if total is None else total + value
    far_3 = box_tile(total)

    def lowered(parent, base, boxes):
        rows = jnp.concatenate(
            [jnp.where(low, parent, 0.0), jnp.where(low, swap_halves(parent), 0.0)], axis=0
        ).astype(BF16)
        product = lax.dot_general(
            rows,
            up_b[base * RANK : (base + boxes) * RANK, :],
            (((1,), (1,)), ((), ())),
            preferred_element_type=F32,
        )
        result = []
        for pair in range(0, boxes, 2):
            even = product[:8, pair * RANK : pair * RANK + LANES]
            odd = product[8:, pair * RANK : pair * RANK + LANES]
            result.append(jnp.where(low, even, swap_halves(odd)))
            result.append(jnp.where(low, swap_halves(even), odd))
        return result

    for copy in sends_f:
        copy.wait_recv()
    field_4 = (parts[0] + parts[1]) + (parts[2] + parts[3])
    rows = jnp.concatenate(
        [jnp.where(low, field_4, 0.0), jnp.where(low, swap_halves(field_4), 0.0)], axis=0
    ).astype(BF16)
    product = lax.dot_general(
        rows,
        up_b[84 * RANK : 85 * RANK, :],
        (((1,), (1,)), ((), ())),
        preferred_element_type=F32,
    )
    product = jnp.concatenate([product, jnp.zeros_like(product)], axis=1)
    field_3 = far_3 + jnp.where(low, product[:8], swap_halves(product[8:]))
    down = lowered(field_3, 80, 4)
    field_2 = [far[640 + 8 * c : 648 + 8 * c, :] + down[c] for c in range(4)]
    field_1 = []
    for p in range(4):
        down = lowered(field_2[p], 64 + 4 * p, 4)
        for c in range(4):
            row = 512 + 8 * (4 * p + c)
            field_1.append(far[row : row + 8, :] + down[c])
    for p in range(16):
        down = lowered(field_1[p], 4 * p, 4)
        for c in range(4):
            box = 4 * p + c
            tiles[pl.ds((box // 8) * 64 + box % 8, 8, stride=8), :] = (
                far[8 * box : 8 * box + 8, :] + down[c]
            )
    for big in range(8):
        for j in range(8):
            row = (big * 8 + j) * 8
            out[big * 8 : big * 8 + 8, j * LANES : (j + 1) * LANES] = tiles[row : row + 8, :]

    for copy in sends_a + sends_b + sends_t + sends_f:
        copy.wait_send()
    all_top(send_m).wait()


def solution(mesh):
    devices = mesh.shape["wide"] * mesh.shape["narrow"]
    tops = devices // 4
    split = P(("wide", "narrow"), None)
    line = P(("wide", "narrow"))
    anywhere = pl.BlockSpec(memory_space=pl.ANY)
    scalars = pl.BlockSpec(memory_space=pltpu.SMEM)
    inside = pl.BlockSpec(memory_space=pltpu.VMEM)
    vmem = pltpu.VMEM
    dma = pltpu.SemaphoreType.DMA

    def body(*arrays):
        return pl.pallas_call(
            functools.partial(kernel, devices),
            out_shape=jax.ShapeDtypeStruct((64, WIDTH), F32),
            in_specs=[anywhere] * 11 + [inside] * 4 + [scalars] * 5,
            out_specs=pl.BlockSpec(memory_space=pltpu.VMEM),
            scratch_shapes=[
                vmem((64, WIDTH), F32),
                vmem((64, BLOCK), BF16),
                vmem((16, BLOCK), BF16),
                vmem((4, BLOCK), BF16),
                vmem((1, BLOCK), BF16),
                vmem((1792, BLOCK), BF16),
                vmem((448, BLOCK), BF16),
                vmem((112, BLOCK), BF16),
                vmem((28, BLOCK), BF16),
                vmem((7, BLOCK), BF16),
                vmem((1792,), jnp.int32),
                vmem((32, BLOCK), F32),
                vmem((16, BLOCK), F32),
                vmem((512, LANES), F32),
                vmem((256, LANES), F32),
                vmem((WIDTH, WIDTH), BF16),
                vmem((WINDOW, 64, WIDTH), BF16),
                vmem((WINDOW, 32, WIDTH), BF16),
                vmem((85 * RANK, LANES), F32),
                vmem((85 * RANK, LANES), BF16),
                vmem((32, LANES), jnp.int32),
                vmem((21 * LANES, LANES), jnp.int32),
                vmem((1792, WIDTH), BF16),
                vmem((84 * 8, LANES), F32),
                vmem((4, 8, LANES), F32),
                vmem((tops, 8, LANES), F32),
                vmem((4, 8, LANES), F32),
                dma((11,)),
                dma((2 * REACH,)),
                dma((WINDOW,)),
                dma((2 * REACH,)),
                dma((WINDOW,)),
                dma((4,)),
                dma((4,)),
                dma,
                dma,
                dma((4,)),
                dma((4,)),
            ],
            compiler_params=pltpu.CompilerParams(
                collective_id=0, has_side_effects=True, vmem_limit_bytes=56 * 1024 * 1024
            ),
        )(*arrays)

    return jax.shard_map(
        body,
        mesh=mesh,
        in_specs=(split,) * 10 + (line,) * 9 + (P(),),
        out_specs=split,
        check_vma=False,
    )
```

```python
import functools

import jax
import jax.numpy as jnp
from jax import lax
from jax.experimental import pallas as pl
from jax.experimental.pallas import tpu as pltpu
from jax.sharding import PartitionSpec as P

RANK = 64
RHS = 16
LIST = 28
REACH = 4
WIDTH = RHS * RANK
BLOCK = RANK * RANK
LANES = 128
SUPER = 4 * LIST
GROUP = 32
WIDE = 2 * SUPER
PIECES = 2
PART = WIDTH // PIECES
WINDOW = 2 * REACH + 1
MESH = pl.DeviceIdType.MESH
BF16 = jnp.bfloat16
F32 = jnp.float32


def low_lanes(shape):
    return lax.broadcasted_iota(jnp.int32, shape, 1) < RANK


def swap_halves(value):
    return pltpu.roll(value, RANK, 1)


def kernel(
    devices,
    moments,
    up_0,
    up_1,
    up_2,
    up_3,
    couple_0,
    couple_1,
    couple_2,
    couple_3,
    couple_4,
    sources_0,
    sources_1,
    sources_2,
    sources_3,
    sources_4,
    counts_0,
    counts_1,
    counts_2,
    counts_3,
    counts_4,
    out,
    mom,
    u0,
    u1,
    u2,
    u3,
    couples,
    c3,
    c4,
    s0,
    pad3,
    pad4,
    tiles,
    rows_b,
    perm,
    win_a,
    win_b,
    up_f,
    up_b,
    lines,
    index,
    hot_0,
    hot_1,
    gathered,
    far,
    terms,
    top,
    parts,
    load_sem,
    send_a,
    recv_a,
    pass_a,
    send_b,
    recv_b,
    pass_b,
    send_t,
    recv_t,
    send_m,
    recv_m,
    send_f,
    recv_f,
):
    tops = devices // 4
    me = lax.axis_index("wide") * 2 + lax.axis_index("narrow")
    member = lax.rem(me, 4)
    group = lax.div(me, 4)
    core = lax.rem(lax.div(me, 2), 2)

    def place(position):
        return (lax.div(position, 2), lax.rem(position, 2))

    def shifted(by):
        return lax.rem(me + by + devices, devices)

    def mate(v):
        return group * 4 + lax.rem(member + v, 4)

    offsets = [o for o in range(-REACH, REACH + 1) if o != 0]

    barrier = pltpu.get_barrier_semaphore()
    for o in offsets:
        pl.semaphore_signal(barrier, inc=1, device_id=place(shifted(o)), device_id_type=MESH)

    def greet(u, carry):
        pl.semaphore_signal(
            barrier, inc=1, device_id=place(shifted(4 * u)), device_id_type=MESH
        )
        return carry

    lax.fori_loop(2, tops - 1, greet, 0)

    loads = [
        (moments, mom),
        (up_0, u0),
        (up_1, u1),
        (up_2, u2),
        (up_3, u3),
        (sources_0, s0),
        (couple_3, c3),
        (couple_4, c4),
        (couple_0, couples.at[pl.ds(0, 1792)]),
        (couple_1, couples.at[pl.ds(1792, 448)]),
        (couple_2, couples.at[pl.ds(2240, 112)]),
    ]
    copies = [
        pltpu.make_async_copy(src, dst, load_sem.at[n]) for n, (src, dst) in enumerate(loads)
    ]
    for copy in copies:
        copy.start()

    def build_perm(j, carry):
        a = lax.broadcasted_iota(jnp.int32, (LANES, WIDTH), 0)
        b = lax.broadcasted_iota(jnp.int32, (LANES, WIDTH), 1)
        wanted = (a % RANK) * RHS + (a // RANK) * 8 + j
        start = pl.multiple_of(j * LANES, LANES)
        perm[pl.ds(start, LANES), :] = jnp.where(wanted == b, 1.0, 0.0).astype(BF16)
        return carry

    lax.fori_loop(0, 8, build_perm, 0)

    copies[0].wait()
    own = jnp.dot(mom[...].astype(BF16), perm[...], preferred_element_type=F32).astype(BF16)
    for h in range(PIECES):
        win_a[h, REACH] = own[:, h * PART : (h + 1) * PART]

    pl.semaphore_wait(barrier, len(offsets) + tops - 3)

    def when(condition, act):
        if condition is None:
            act()
        else:
            pl.when(condition)(act)

    def direct(window, send, recv):
        result = []
        for n, o in enumerate(offsets):
            target = shifted(o)
            target_core = lax.rem(lax.div(target, 2), 2)
            condition = None if o == -1 else target_core == (0 if o > 0 else 1)
            copy = pltpu.make_async_remote_copy(
                src_ref=window.at[REACH],
                dst_ref=window.at[REACH - o],
                send_sem=send.at[n],
                recv_sem=recv.at[REACH - o],
                device_id=place(target),
                device_id_type=MESH,
            )
            result.append((condition, copy))
        return result

    def passes(window, send, recv, slots):
        result = []
        for which, by in ((0, -2), (1, 2)):
            for slot in slots[which]:
                copy = pltpu.make_async_remote_copy(
                    src_ref=window.at[slot],
                    dst_ref=window.at[slot + by],
                    send_sem=send.at[slot],
                    recv_sem=recv.at[slot + by],
                    device_id=place(shifted(-by)),
                    device_id_type=MESH,
                )
                result.append((core == which, copy))
        return result

    def own_rows(window, send, recv):
        return passes(window, send, recv, ([REACH], [REACH]))

    def shared_rows(window, send, recv):
        return passes(window, send, recv, ([2, 3, 5], [5, 6]))

    def start(copies):
        for condition, copy in copies:
            when(condition, copy.start)

    def sent(copies):
        for condition, copy in copies:
            when(condition, copy.wait_send)

    def arrived(window, recv, slots):
        for which in (0, 1):
            for slot in slots[which]:
                copy = pltpu.make_async_copy(window.at[slot], window.at[slot], recv.at[slot])
                when(core == which, copy.wait)

    def arrived_direct(window, recv):
        arrived(window, recv, ([0, 1, 2, 3, 5], [5, 6, 7, 8]))

    def arrived_passed(window, recv):
        arrived(window, recv, ([6, 7, 8], [0, 1, 2, 3]))

    all_sends = []
    for h in range(PIECES):
        for copies_h in (
            direct(win_a.at[h], send_a.at[h], recv_a.at[h]),
            own_rows(win_a.at[h], pass_a.at[h], recv_a.at[h]),
        ):
            start(copies_h)
            all_sends += copies_h

    for n in range(1, 5):
        copies[n].wait()
    bases = [0, 64, 80, 84]

    def spread(m, carry):
        lane = pl.ds(pl.multiple_of(m * LANES, LANES), LANES)
        for source, base, boxes in ((u0, 0, 64), (u1, 64, 16), (u2, 80, 4), (u3, 84, 1)):
            block = source[:, lane].astype(F32)
            other = swap_halves(block)
            step = min(boxes, 8)
            for first in range(0, boxes, step):
                for kp, value in ((0, block), (1, other)):
                    start = (base + first) * RANK + 2 * m + kp
                    piece = value[first : first + step]
                    if step > 1:
                        up_f[pl.ds(start, step, stride=RANK), :] = piece
                    else:
                        up_f[pl.ds(start, 1), :] = piece
        return carry

    lax.fori_loop(0, 32, spread, 0)

    def narrowed(n, carry):
        rows = pl.ds(pl.multiple_of(n * 320, 320), 320)
        up_b[rows, :] = up_f[rows, :].astype(BF16)
        return carry

    lax.fori_loop(0, 17, narrowed, 0)

    for big in range(8):
        for j in range(8):
            tiles[pl.ds((big * 8 + j) * 8, 8), :] = mom[
                big * 8 : big * 8 + 8, j * LANES : (j + 1) * LANES
            ]

    low = low_lanes((8, LANES))

    def beside(first, second):
        even = jnp.where(low, first, swap_halves(second))
        odd = jnp.where(low, swap_halves(first), second)
        return jnp.concatenate([even, odd], axis=0)

    def lifted(children, base):
        left = beside(children[0], children[1])
        right = beside(children[2], children[3])
        rows = jnp.concatenate([left, right], axis=1).astype(BF16)
        product = jnp.dot(
            rows, up_b[base * RANK : (base + 4) * RANK, :], preferred_element_type=F32
        )
        return jnp.where(low, product[:8], swap_halves(product[8:]))

    def tile_of(box):
        return tiles[pl.ds((box // 8) * 64 + box % 8, 8, stride=8), :]

    level_1 = [lifted([tile_of(4 * p + c) for c in range(4)], 4 * p) for p in range(16)]
    level_2 = [lifted(level_1[4 * p : 4 * p + 4], 64 + 4 * p) for p in range(4)]
    level_3 = lifted(level_2, 80)
    alone = jnp.concatenate([level_3, swap_halves(level_3)], axis=0)[:, :RANK].astype(BF16)
    product = jnp.dot(alone, up_b[84 * RANK : 85 * RANK, :], preferred_element_type=F32)
    terms[0] = jnp.where(low, product[:8], swap_halves(product[8:]))

    def to_mates(buffer, send, recv):
        return [
            pltpu.make_async_remote_copy(
                src_ref=buffer.at[0],
                dst_ref=buffer.at[4 - v],
                send_sem=send.at[v],
                recv_sem=recv.at[4 - v],
                device_id=place(mate(v)),
                device_id_type=MESH,
            )
            for v in (1, 2, 3)
        ]

    sends_t = to_mates(terms, send_t, recv_t)
    for copy in sends_t:
        copy.start()

    rows_b[...] = jnp.zeros_like(rows_b)
    for row, value in enumerate(level_1 + level_2 + [level_3]):
        rows_b[pl.ds((row // 8) * 64 + row % 8, 8, stride=8), :] = value
    natural = jnp.concatenate(
        [
            jnp.concatenate(
                [rows_b[(big * 8 + j) * 8 : (big * 8 + j) * 8 + 8, :] for j in range(8)], axis=1
            )
            for big in range(4)
        ],
        axis=0,
    ).astype(BF16)
    win_b[REACH] = jnp.dot(natural, perm[...], preferred_element_type=F32).astype(BF16)
    for copies_b in (direct(win_b, send_b, recv_b), own_rows(win_b, pass_b, recv_b)):
        start(copies_b)
        all_sends += copies_b

    copies[5].wait()
    first = me - REACH
    for j in range(14):
        lines[j : j + 1, :] = s0[pl.ds(j * LANES, LANES)].reshape(1, LANES) - first * 64
    lines[14:32, :] = jnp.zeros((18, LANES), jnp.int32)
    for j in range(4):
        length = min(LANES, 448 - j * LANES)
        local = sources_1[pl.ds(j * LANES, length)].reshape(1, length) - first * 16
        lines[14 + j : 15 + j, :length] = (local >> 4) * 32 + (local & 15)
    local = sources_2[...].reshape(1, 112) - first * 4
    lines[18:19, :112] = (local >> 2) * 32 + 16 + (local & 3)
    lines[19:20, :28] = (sources_3[...].reshape(1, 28) - first) * 32 + 20
    lines[20:21, :7] = (sources_4[...].reshape(1, 7) - group) & (tops - 1)
    columns = lines[...].T
    places = [j * LANES for j in range(18)] + [2240, 2352, 2560]
    for j, row in enumerate(places):
        index[row : row + LANES, :] = jnp.broadcast_to(columns[:, j : j + 1], (LANES, LANES))

    slot = lax.broadcasted_iota(jnp.int32, (SUPER, LANES), 0)

    def drop_invalid(base, counts):
        limit = counts[3] + 3 * LIST
        for b in (2, 1, 0):
            limit = jnp.where(slot < (b + 1) * LIST, counts[b] + b * LIST, limit)
        rows = pl.ds(base, SUPER)
        index[rows, :] = jnp.where(slot < limit, index[rows, :], -1)

    def drop_level(first_row, counts_ref, n):
        def step(n, carry):
            base = pl.multiple_of(first_row + n * SUPER, 16)
            drop_invalid(base, [counts_ref[4 * n + b] for b in range(4)])
            return carry

        lax.fori_loop(0, n, step, 0)

    drop_level(0, counts_0, 16)
    drop_level(1792, counts_1, 4)
    drop_level(2240, counts_2, 1)
    few = lax.broadcasted_iota(jnp.int32, (48, LANES), 0)
    index[2352:2400, :] = jnp.where(few < counts_3[0], index[2352:2400, :], -1)
    left = jnp.minimum(counts_4[group] - member * 7, 7)
    index[2560:2576, :] = jnp.where(few[:16] < left, index[2560:2576, :], -1)

    def one_hot(from_row, count, width):
        place_of = index[pl.ds(from_row, count), :]
        lane = lax.broadcasted_iota(jnp.int32, (count, LANES), 1)
        hot = [
            jnp.where(place_of == lane + first_lane, 1.0, 0.0).astype(BF16)[
                :, : min(LANES, width - first_lane)
            ]
            for first_lane in range(0, width, LANES)
        ]
        return jnp.concatenate(hot, axis=1) if len(hot) > 1 else hot[0]

    def mark_0(n, carry):
        row = pl.multiple_of(n * LANES, LANES)
        hot_0[pl.ds(row, LANES), :] = one_hot(row, LANES, WINDOW * 64)
        return carry

    lax.fori_loop(0, 14, mark_0, 0)

    def mark_1(n, carry):
        row = pl.multiple_of(n * 304, 16)
        hot_1[pl.ds(row, 304), :] = one_hot(pl.multiple_of(1792 + row, 16), 304, WINDOW * 32)
        return carry

    lax.fori_loop(0, 2, mark_1, 0)

    for copy in sends_t:
        copy.wait_recv()
    top[0] = (terms[0] + terms[1]) + (terms[2] + terms[3])

    def to_top(u):
        return pltpu.make_async_remote_copy(
            src_ref=top.at[0],
            dst_ref=top.at[tops - u],
            send_sem=send_m,
            recv_sem=recv_m,
            device_id=place(shifted(4 * u)),
            device_id_type=MESH,
        )

    def send_top(u, carry):
        to_top(u).start()
        return carry

    lax.fori_loop(1, tops, send_top, 0)

    def turned_few(rows):
        stack = jnp.concatenate(
            [rows[:, i * LANES : (i + 1) * LANES] for i in range(8)], axis=0
        )
        across = stack.T
        return jnp.concatenate([across[32 * m : 32 * m + 32] for m in range(4)], axis=1)

    def stacked_few(rows):
        return jnp.concatenate(
            [
                rows[:, (4 * i + m) * LANES : (4 * i + m + 1) * LANES]
                for m in range(4)
                for i in range(8)
            ],
            axis=0,
        )

    def turned(rows):
        stack = jnp.concatenate(
            [rows[:, i * LANES : (i + 1) * LANES] for i in range(4)], axis=0
        )
        across = stack.T
        return jnp.concatenate([across[32 * m : 32 * m + 32] for m in range(4)], axis=1)

    def stacked(rows):
        return jnp.concatenate(
            [
                rows[:, (4 * i + m) * LANES : (4 * i + m + 1) * LANES]
                for m in range(4)
                for i in range(4)
            ],
            axis=0,
        )

    def box_tile(value):
        a, b, c, d = (value[8 * n : 8 * n + 8] for n in range(4))
        return jnp.where(low, a, d) + swap_halves(jnp.where(low, b, c))

    half = BLOCK // PIECES

    def far_part(h, rows_from, couple_from, far_from, groups, boxes):
        totals = [None] * boxes
        lane_slot = lax.broadcasted_iota(jnp.int32, (32, 512), 1) % GROUP
        for g in range(groups):
            left = turned(gathered[pl.ds(rows_from + GROUP * g, GROUP), :])
            right = stacked(
                couples[pl.ds(couple_from + GROUP * g, GROUP), h * half : (h + 1) * half]
            )
            touched = [
                b
                for b in range(boxes)
                if b * LIST < GROUP * (g + 1) and (b + 1) * LIST > GROUP * g
            ]
            if len(touched) == 2:
                border = touched[1] * LIST - GROUP * g
                zero = jnp.zeros_like(left)
                left = jnp.concatenate(
                    [
                        jnp.where(lane_slot < border, left, zero),
                        jnp.where(lane_slot < border, zero, left),
                    ],
                    axis=0,
                )
            value = jnp.dot(left, right, preferred_element_type=F32)
            for n, b in enumerate(touched):
                part = value[32 * n : 32 * n + 32]
                totals[b] = part if totals[b] is None else totals[b] + part
        for b in range(boxes):
            rows = pl.ds(far_from + 8 * b, 8)
            if h == 0:
                far[rows, :] = box_tile(totals[b])
            else:
                far[rows, :] += box_tile(totals[b])

    def gather_0(h):
        sources = win_a[h].reshape(WINDOW * 64, PART)

        def step(n, carry):
            rows = pl.ds(pl.multiple_of(n * 448, 448), 448)
            gathered[rows, :] = jnp.dot(
                hot_0[rows, :], sources, preferred_element_type=F32
            ).astype(BF16)
            return carry

        lax.fori_loop(0, 4, step, 0)

    def far_0(h, first, last):
        def step(n, carry):
            row = pl.multiple_of(n * WIDE, WIDE)
            far_part(h, row, row, pl.multiple_of(n * 64, 64), 7, 8)
            return carry

        lax.fori_loop(first, last, step, 0)

    arrived_direct(win_a.at[0], recv_a.at[0])
    shared = shared_rows(win_a.at[0], pass_a.at[0], recv_a.at[0])
    start(shared)
    all_sends += shared
    copies[6].wait()
    copies[7].wait()
    pad4[...] = jnp.zeros_like(pad4)
    pad4[0:7, :] = c4[...].astype(F32)
    pad3[...] = jnp.zeros_like(pad3)
    pad3[0:28, :] = c3[...].astype(F32)
    couples[2352:2384, :] = pad3[...].astype(BF16)
    couples[2384:2400, :] = jnp.zeros((16, BLOCK), BF16)
    arrived_passed(win_a.at[0], recv_a.at[0])
    gather_0(0)
    copies[8].wait()
    far_0(0, 0, 4)
    arrived_direct(win_a.at[1], recv_a.at[1])
    shared = shared_rows(win_a.at[1], pass_a.at[1], recv_a.at[1])
    start(shared)
    all_sends += shared
    far_0(0, 4, 8)

    def all_top(n):
        return pltpu.make_async_copy(
            top.at[pl.ds(1, tops - 1)], top.at[pl.ds(1, tops - 1)], n
        )

    all_top(recv_m).wait()
    count = max(tops, 8)
    if tops < 8:
        tiles[0:512, :] = jnp.zeros((512, LANES), F32)
    for row in range(tops):
        tiles[pl.ds((row // 8) * 64 + row % 8, 8, stride=8), :] = top[row]
    natural = jnp.concatenate(
        [
            jnp.concatenate(
                [tiles[(big * 8 + j) * 8 : (big * 8 + j) * 8 + 8, :] for j in range(8)], axis=1
            )
            for big in range(count // 8)
        ],
        axis=0,
    ).astype(BF16)
    top_rows = jnp.dot(natural, perm[...], preferred_element_type=F32).astype(BF16)
    rows = jnp.dot(one_hot(2560, 16, count), top_rows, preferred_element_type=F32)
    left = turned_few(rows.astype(BF16))
    right = stacked_few(pad4[...].astype(BF16))
    parts[0] = box_tile(jnp.dot(left, right, preferred_element_type=F32))
    sends_f = to_mates(parts, send_f, recv_f)
    for copy in sends_f:
        copy.start()

    arrived_passed(win_a.at[1], recv_a.at[1])
    gather_0(1)
    far_0(1, 0, 4)
    arrived_direct(win_b, recv_b)
    shared = shared_rows(win_b, pass_b, recv_b)
    start(shared)
    all_sends += shared
    far_0(1, 4, 8)

    arrived_passed(win_b, recv_b)
    copies[9].wait()
    copies[10].wait()
    for h in range(PIECES):
        gathered[0:608, :] = jnp.dot(
            hot_1[...],
            win_b[:, :, h * PART : (h + 1) * PART].reshape(WINDOW * 32, PART),
            preferred_element_type=F32,
        ).astype(BF16)

        def far_1(n, carry):
            row = pl.multiple_of(n * WIDE, WIDE)
            far_part(h, row, 1792 + row, 512 + pl.multiple_of(n * 64, 64), 7, 8)
            return carry

        lax.fori_loop(0, 2, far_1, 0)
        far_part(h, 448, 2240, 640, 5, 5)

    def lowered(parent, base, boxes):
        rows = jnp.concatenate(
            [jnp.where(low, parent, 0.0), jnp.where(low, swap_halves(parent), 0.0)], axis=0
        ).astype(BF16)
        product = lax.dot_general(
            rows,
            up_b[base * RANK : (base + boxes) * RANK, :],
            (((1,), (1,)), ((), ())),
            preferred_element_type=F32,
        )
        result = []
        for pair in range(0, boxes, 2):
            even = product[:8, pair * RANK : pair * RANK + LANES]
            odd = product[8:, pair * RANK : pair * RANK + LANES]
            result.append(jnp.where(low, even, swap_halves(odd)))
            result.append(jnp.where(low, swap_halves(even), odd))
        return result

    for copy in sends_f:
        copy.wait_recv()
    field_4 = (parts[0] + parts[1]) + (parts[2] + parts[3])
    rows = jnp.concatenate(
        [jnp.where(low, field_4, 0.0), jnp.where(low, swap_halves(field_4), 0.0)], axis=0
    ).astype(BF16)
    product = lax.dot_general(
        rows,
        up_b[84 * RANK : 85 * RANK, :],
        (((1,), (1,)), ((), ())),
        preferred_element_type=F32,
    )
    product = jnp.concatenate([product, jnp.zeros_like(product)], axis=1)
    field_3 = far[672:680, :] + jnp.where(low, product[:8], swap_halves(product[8:]))
    down = lowered(field_3, 80, 4)
    field_2 = [far[640 + 8 * c : 648 + 8 * c, :] + down[c] for c in range(4)]
    field_1 = []
    for p in range(4):
        down = lowered(field_2[p], 64 + 4 * p, 4)
        for c in range(4):
            row = 512 + 8 * (4 * p + c)
            field_1.append(far[row : row + 8, :] + down[c])
    for p in range(16):
        down = lowered(field_1[p], 4 * p, 4)
        for c in range(4):
            box = 4 * p + c
            tiles[pl.ds((box // 8) * 64 + box % 8, 8, stride=8), :] = (
                far[8 * box : 8 * box + 8, :] + down[c]
            )
    for big in range(8):
        for j in range(8):
            row = (big * 8 + j) * 8
            out[big * 8 : big * 8 + 8, j * LANES : (j + 1) * LANES] = tiles[row : row + 8, :]

    for copy in sends_t + sends_f:
        copy.wait_send()
    sent(all_sends)
    all_top(send_m).wait()


def solution(mesh):
    devices = mesh.shape["wide"] * mesh.shape["narrow"]
    tops = devices // 4
    split = P(("wide", "narrow"), None)
    line = P(("wide", "narrow"))
    anywhere = pl.BlockSpec(memory_space=pl.ANY)
    scalars = pl.BlockSpec(memory_space=pltpu.SMEM)
    inside = pl.BlockSpec(memory_space=pltpu.VMEM)
    vmem = pltpu.VMEM
    dma = pltpu.SemaphoreType.DMA

    def body(*arrays):
        return pl.pallas_call(
            functools.partial(kernel, devices),
            out_shape=jax.ShapeDtypeStruct((64, WIDTH), F32),
            in_specs=[anywhere] * 11 + [inside] * 4 + [scalars] * 5,
            out_specs=pl.BlockSpec(memory_space=pltpu.VMEM),
            scratch_shapes=[
                vmem((64, WIDTH), F32),
                vmem((64, BLOCK), BF16),
                vmem((16, BLOCK), BF16),
                vmem((4, BLOCK), BF16),
                vmem((1, BLOCK), BF16),
                vmem((2400, BLOCK), BF16),
                vmem((28, BLOCK), BF16),
                vmem((7, BLOCK), BF16),
                vmem((1792,), jnp.int32),
                vmem((32, BLOCK), F32),
                vmem((16, BLOCK), F32),
                vmem((512, LANES), F32),
                vmem((256, LANES), F32),
                vmem((WIDTH, WIDTH), BF16),
                vmem((PIECES, WINDOW, 64, PART), BF16),
                vmem((WINDOW, 32, WIDTH), BF16),
                vmem((85 * RANK, LANES), F32),
                vmem((85 * RANK, LANES), BF16),
                vmem((32, LANES), jnp.int32),
                vmem((21 * LANES, LANES), jnp.int32),
                vmem((1792, WINDOW * 64), BF16),
                vmem((608, WINDOW * 32), BF16),
                vmem((1792, PART), BF16),
                vmem((85 * 8, LANES), F32),
                vmem((4, 8, LANES), F32),
                vmem((tops, 8, LANES), F32),
                vmem((4, 8, LANES), F32),
                dma((11,)),
                dma((PIECES, 2 * REACH)),
                dma((PIECES, WINDOW)),
                dma((PIECES, WINDOW)),
                dma((2 * REACH,)),
                dma((WINDOW,)),
                dma((WINDOW,)),
                dma((4,)),
                dma((4,)),
                dma,
                dma,
                dma((4,)),
                dma((4,)),
            ],
            compiler_params=pltpu.CompilerParams(
                collective_id=0, has_side_effects=True, vmem_limit_bytes=56 * 1024 * 1024
            ),
        )(*arrays)

    return jax.shard_map(
        body,
        mesh=mesh,
        in_specs=(split,) * 10 + (line,) * 9 + (P(),),
        out_specs=split,
        check_vma=False,
    )
```

```python
import functools

import jax
import jax.numpy as jnp
from jax import lax
from jax.experimental import pallas as pl
from jax.experimental.pallas import tpu as pltpu
from jax.sharding import PartitionSpec as P

RANK = 64
RHS = 16
LIST = 28
REACH = 4
WIDTH = RHS * RANK
BLOCK = RANK * RANK
LANES = 128
SUPER = 4 * LIST
GROUP = 32
WIDE = 2 * SUPER
PIECES = 2
PART = WIDTH // PIECES
WINDOW = 2 * REACH + 1
MESH = pl.DeviceIdType.MESH
BF16 = jnp.bfloat16
F32 = jnp.float32


def low_lanes(shape):
    return lax.broadcasted_iota(jnp.int32, shape, 1) < RANK


def swap_halves(value):
    return pltpu.roll(value, RANK, 1)


def kernel(
    devices,
    planes,
    moments,
    up_0,
    up_1,
    up_2,
    up_3,
    couple_0,
    couple_1,
    couple_2,
    couple_3,
    couple_4,
    sources_0,
    sources_1,
    sources_2,
    sources_3,
    sources_4,
    counts_0,
    counts_1,
    counts_2,
    counts_3,
    counts_4,
    out,
    mom,
    u0,
    u1,
    u2,
    u3,
    couples,
    c3,
    c4,
    s0,
    pad3,
    pad4,
    tiles,
    rows_b,
    perm,
    win_a,
    win_b,
    few_up,
    by_pair,
    by_row,
    up_b,
    lines,
    index,
    hot_0,
    hot_1,
    gathered,
    far,
    terms,
    top,
    slots_4,
    load_sem,
    send_a,
    recv_a,
    pass_a,
    send_b,
    recv_b,
    pass_b,
    send_t,
    recv_t,
    send_z,
    recv_z,
    send_y,
    recv_y,
    send_s,
    recv_s,
    send_c,
    recv_c,
):
    rows = devices // 8 // planes
    me = lax.axis_index("wide") * 2 + lax.axis_index("narrow")
    member = lax.rem(me, 4)
    group = lax.div(me, 4)
    core = lax.rem(lax.div(me, 2), 2)
    seat = lax.rem(me, 8)
    my_row = lax.div(me, 8)
    z, y = lax.rem(my_row, rows), lax.div(my_row, rows)
    opposite = me + 1 - 2 * lax.rem(me, 2)
    sibling = me + 2 - 4 * core

    def place(position):
        return (lax.div(position, 2), lax.rem(position, 2))

    def mate(v):
        return group * 4 + lax.rem(member + v, 4)

    def row_mate(v):
        return my_row * 8 + lax.rem(seat + v, 8)

    def along_z(k):
        return (y * rows + lax.rem(z + k, rows)) * 8 + seat

    def along_y(k):
        return (lax.rem(y + k, planes) * rows + z) * 8 + seat

    def exists(o):
        return jnp.logical_and(me + o >= 0, me + o < devices)

    offsets = [o for o in range(-REACH, REACH + 1) if o != 0]

    for o in offsets:

        @pl.when(jnp.logical_not(exists(o)))
        def _():
            for h in range(PIECES):
                win_a[h, REACH + o] = jnp.zeros((64, PART), BF16)
            win_b[REACH + o] = jnp.zeros((32, WIDTH), BF16)

    barrier = pltpu.get_barrier_semaphore()

    def greet(position):
        pl.semaphore_signal(barrier, inc=1, device_id=place(position), device_id_type=MESH)

    greeted = jnp.int32(rows - 1 + planes - 1)
    for o in offsets + [-7, -6, -5, 5, 6, 7]:
        known = exists(o)
        if abs(o) > REACH:
            known = jnp.logical_and(seat + o >= 0, seat + o < 8)
        pl.when(known)(functools.partial(greet, me + o))
        greeted = greeted + known.astype(jnp.int32)
    for k in range(1, rows):
        greet(along_z(k))
    for k in range(1, planes):
        greet(along_y(k))

    loads = [
        (moments, mom),
        (up_0, u0),
        (up_1, u1),
        (up_2, u2),
        (up_3, u3),
        (sources_0, s0),
        (couple_3, c3),
        (couple_4, c4.at[member]),
        (couple_0, couples.at[pl.ds(0, 1792)]),
        (couple_1, couples.at[pl.ds(1792, 448)]),
        (couple_2, couples.at[pl.ds(2240, 112)]),
    ]
    copies = [
        pltpu.make_async_copy(src, dst, load_sem.at[n]) for n, (src, dst) in enumerate(loads)
    ]
    for copy in copies:
        copy.start()

    def build_perm(j, carry):
        a = lax.broadcasted_iota(jnp.int32, (LANES, WIDTH), 0)
        b = lax.broadcasted_iota(jnp.int32, (LANES, WIDTH), 1)
        wanted = (a % RANK) * RHS + (a // RANK) * 8 + j
        start = pl.multiple_of(j * LANES, LANES)
        perm[pl.ds(start, LANES), :] = jnp.where(wanted == b, 1.0, 0.0).astype(BF16)
        return carry

    lax.fori_loop(0, 8, build_perm, 0)

    a = lax.broadcasted_iota(jnp.int32, (512, 512), 0)
    b = lax.broadcasted_iota(jnp.int32, (512, 512), 1)
    by_pair[...] = jnp.where(b == (a % 32) * 16 + a // 32, 1.0, 0.0).astype(BF16)
    a = lax.broadcasted_iota(jnp.int32, (256, 256), 0)
    b = lax.broadcasted_iota(jnp.int32, (256, 256), 1)
    by_row[...] = jnp.where(b == (a % 2) * 128 + a // 2, 1.0, 0.0).astype(BF16)

    copies[0].wait()
    own = jnp.dot(mom[...].astype(BF16), perm[...], preferred_element_type=F32).astype(BF16)
    for h in range(PIECES):
        win_a[h, REACH] = own[:, h * PART : (h + 1) * PART]

    pl.semaphore_wait(barrier, greeted)

    def when(condition, act):
        pl.when(condition)(act)

    def direct(window, send, recv):
        result = []
        for n, o in enumerate(offsets):
            target = me + o
            target_core = lax.rem(lax.div(target + 4, 2), 2)
            condition = exists(o)
            if o != -1:
                condition = jnp.logical_and(condition, target_core == (0 if o > 0 else 1))
            copy = pltpu.make_async_remote_copy(
                src_ref=window.at[REACH],
                dst_ref=window.at[REACH - o],
                send_sem=send.at[n],
                recv_sem=recv.at[REACH - o],
                device_id=place(target),
                device_id_type=MESH,
            )
            result.append((condition, copy))
        return result

    def passes(window, send, recv, slots):
        result = []
        for which, by in ((0, -2), (1, 2)):
            for slot in slots[which]:
                copy = pltpu.make_async_remote_copy(
                    src_ref=window.at[slot],
                    dst_ref=window.at[slot + by],
                    send_sem=send.at[slot],
                    recv_sem=recv.at[slot + by],
                    device_id=place(me - by),
                    device_id_type=MESH,
                )
                result.append((jnp.logical_and(core == which, exists(slot - REACH)), copy))
        return result

    def own_rows(window, send, recv):
        return passes(window, send, recv, ([REACH], [REACH]))

    def shared_rows(window, send, recv):
        return passes(window, send, recv, ([2, 3, 5], [5, 6]))

    def start(copies):
        for condition, copy in copies:
            when(condition, copy.start)

    def sent(copies):
        for condition, copy in copies:
            when(condition, copy.wait_send)

    def arrived(window, recv, slots):
        for which in (0, 1):
            for slot in slots[which]:
                copy = pltpu.make_async_copy(window.at[slot], window.at[slot], recv.at[slot])
                when(jnp.logical_and(core == which, exists(slot - REACH)), copy.wait)

    def arrived_direct(window, recv):
        arrived(window, recv, ([0, 1, 2, 3, 5], [5, 6, 7, 8]))

    def arrived_passed(window, recv):
        arrived(window, recv, ([6, 7, 8], [0, 1, 2, 3]))

    def send_part(h):
        result = direct(win_a.at[h], send_a.at[h], recv_a.at[h])
        result += own_rows(win_a.at[h], pass_a.at[h], recv_a.at[h])
        start(result)
        return result

    all_sends = send_part(0)

    def whole(ref, to, send_sem, recv_sem):
        return pltpu.make_async_remote_copy(
            src_ref=ref,
            dst_ref=ref,
            send_sem=send_sem,
            recv_sem=recv_sem,
            device_id=place(to),
            device_id_type=MESH,
        )

    for n in range(1, 5):
        copies[n].wait()
    few_up[...] = jnp.zeros_like(few_up)
    few_up[0:4, :] = u2[...].astype(F32)
    few_up[4:5, :] = u3[...].astype(F32)
    blocks = [u0[16 * n : 16 * n + 16, :] for n in range(4)]
    blocks += [u1[...], few_up[...].astype(BF16)]
    columns = jnp.concatenate(
        [
            jnp.concatenate([block[:, m * LANES : (m + 1) * LANES] for m in range(32)], axis=0)
            for block in blocks
        ],
        axis=1,
    )
    by_box = jnp.dot(by_pair[...], columns, preferred_element_type=F32)
    for n in range(6):
        quads = []
        for p in range(4 if n < 5 else 2):
            one = by_box[128 * p : 128 * p + 128, n * LANES : (n + 1) * LANES]
            quads.append(jnp.concatenate([one, swap_halves(one)], axis=0).astype(BF16))
        upright = jnp.dot(
            by_row[...], jnp.concatenate(quads, axis=1), preferred_element_type=F32
        ).astype(BF16)
        for p in range(len(quads)):
            base = (4 * n + p) * 256
            up_b[base : base + 256, :] = upright[:, p * LANES : (p + 1) * LANES]

    for big in range(8):
        for j in range(8):
            tiles[pl.ds((big * 8 + j) * 8, 8), :] = mom[
                big * 8 : big * 8 + 8, j * LANES : (j + 1) * LANES
            ]

    low = low_lanes((8, LANES))

    def beside(first, second):
        even = jnp.where(low, first, swap_halves(second))
        odd = jnp.where(low, swap_halves(first), second)
        return jnp.concatenate([even, odd], axis=0)

    def lifted(children, base):
        left = beside(children[0], children[1])
        right = beside(children[2], children[3])
        rows = jnp.concatenate([left, right], axis=1).astype(BF16)
        product = jnp.dot(
            rows, up_b[base * RANK : (base + 4) * RANK, :], preferred_element_type=F32
        )
        return jnp.where(low, product[:8], swap_halves(product[8:]))

    def tile_of(box):
        return tiles[pl.ds((box // 8) * 64 + box % 8, 8, stride=8), :]

    level_1 = [lifted([tile_of(4 * p + c) for c in range(4)], 4 * p) for p in range(16)]
    level_2 = [lifted(level_1[4 * p : 4 * p + 4], 64 + 4 * p) for p in range(4)]
    level_3 = lifted(level_2, 80)
    alone = jnp.concatenate([level_3, swap_halves(level_3)], axis=0)[:, :RANK].astype(BF16)
    product = jnp.dot(alone, up_b[84 * RANK : 85 * RANK, :], preferred_element_type=F32)
    terms[seat] = jnp.where(low, product[:8], swap_halves(product[8:]))

    sends_t = [
        whole(terms.at[seat], row_mate(v), send_t.at[v], recv_t.at[8 - v]) for v in range(1, 8)
    ]
    for copy in sends_t:
        copy.start()

    all_sends += send_part(1)

    rows_b[...] = jnp.zeros_like(rows_b)
    for row, value in enumerate(level_1 + level_2 + [level_3]):
        rows_b[pl.ds((row // 8) * 64 + row % 8, 8, stride=8), :] = value
    natural = jnp.concatenate(
        [
            jnp.concatenate(
                [rows_b[(big * 8 + j) * 8 : (big * 8 + j) * 8 + 8, :] for j in range(8)], axis=1
            )
            for big in range(4)
        ],
        axis=0,
    ).astype(BF16)
    win_b[REACH] = jnp.dot(natural, perm[...], preferred_element_type=F32).astype(BF16)

    copies[5].wait()
    first = me - REACH
    for j in range(14):
        lines[j : j + 1, :] = s0[pl.ds(j * LANES, LANES)].reshape(1, LANES) - first * 64
    lines[14:32, :] = jnp.zeros((18, LANES), jnp.int32)
    for j in range(4):
        length = min(LANES, 448 - j * LANES)
        local = sources_1[pl.ds(j * LANES, length)].reshape(1, length) - first * 16
        lines[14 + j : 15 + j, :length] = (local >> 4) * 32 + (local & 15)
    local = sources_2[...].reshape(1, 112) - first * 4
    lines[18:19, :112] = (local >> 2) * 32 + 16 + (local & 3)
    lines[19:20, :28] = (sources_3[...].reshape(1, 28) - first) * 32 + 20
    columns = lines[...].T
    places = [j * LANES for j in range(18)] + [2240, 2352]
    for j, row in enumerate(places):
        index[row : row + LANES, :] = jnp.broadcast_to(columns[:, j : j + 1], (LANES, LANES))

    slot = lax.broadcasted_iota(jnp.int32, (SUPER, LANES), 0)

    def drop_invalid(base, counts):
        limit = counts[3] + 3 * LIST
        for b in (2, 1, 0):
            limit = jnp.where(slot < (b + 1) * LIST, counts[b] + b * LIST, limit)
        rows = pl.ds(base, SUPER)
        index[rows, :] = jnp.where(slot < limit, index[rows, :], -1)

    def drop_level(first_row, counts_ref, n):
        def step(n, carry):
            base = pl.multiple_of(first_row + n * SUPER, 16)
            drop_invalid(base, [counts_ref[4 * n + b] for b in range(4)])
            return carry

        lax.fori_loop(0, n, step, 0)

    drop_level(0, counts_0, 16)
    drop_level(1792, counts_1, 4)
    drop_level(2240, counts_2, 1)
    few = lax.broadcasted_iota(jnp.int32, (48, LANES), 0)
    index[2352:2400, :] = jnp.where(few < counts_3[0], index[2352:2400, :], -1)

    def one_hot(from_row, count, width):
        place_of = index[pl.ds(from_row, count), :]
        lane = lax.broadcasted_iota(jnp.int32, (count, LANES), 1)
        hot = [
            jnp.where(place_of == lane + first_lane, 1.0, 0.0).astype(BF16)[
                :, : min(LANES, width - first_lane)
            ]
            for first_lane in range(0, width, LANES)
        ]
        return jnp.concatenate(hot, axis=1) if len(hot) > 1 else hot[0]

    def mark_0(n, carry):
        row = pl.multiple_of(n * LANES, LANES)
        hot_0[pl.ds(row, LANES), :] = one_hot(row, LANES, WINDOW * 64)
        return carry

    lax.fori_loop(0, 14, mark_0, 0)

    def mark_1(n, carry):
        row = pl.multiple_of(n * 304, 16)
        hot_1[pl.ds(row, 304), :] = one_hot(pl.multiple_of(1792 + row, 16), 304, WINDOW * 32)
        return carry

    lax.fori_loop(0, 2, mark_1, 0)

    for v in range(1, 8):
        pltpu.make_async_copy(terms.at[0], terms.at[0], recv_t.at[v]).wait()
    for n in range(2):
        four = [terms[4 * n + c] for c in range(4)]
        top[y, z, n] = (four[0] + four[1]) + (four[2] + four[3])
    sends_z = [
        whole(top.at[y, z], along_z(k), send_z.at[k], recv_z.at[rows - k])
        for k in range(1, rows)
    ]
    for copy in sends_z:
        copy.start()
    slots_4[member] = jnp.zeros((8, LANES), jnp.int32)
    slots_4[member, 0:1, :7] = sources_4[...].reshape(1, 7)
    copies[7].wait()
    sends_s = [
        whole(slots_4.at[member], mate(v), send_s.at[v], recv_s.at[4 - v]) for v in (1, 2, 3)
    ]
    sends_c = [
        whole(c4.at[member], opposite, send_c.at[0], recv_c.at[0]),
        whole(c4.at[member], sibling, send_c.at[1], recv_c.at[1]),
    ]
    for copy in sends_s + sends_c:
        copy.start()


    for copies_b in (direct(win_b, send_b, recv_b), own_rows(win_b, pass_b, recv_b)):
        start(copies_b)
        all_sends += copies_b

    def turned(rows):
        stack = jnp.concatenate(
            [rows[:, i * LANES : (i + 1) * LANES] for i in range(4)], axis=0
        )
        across = stack.T
        return jnp.concatenate([across[32 * m : 32 * m + 32] for m in range(4)], axis=1)

    def stacked(rows):
        return jnp.concatenate(
            [
                rows[:, (4 * i + m) * LANES : (4 * i + m + 1) * LANES]
                for m in range(4)
                for i in range(4)
            ],
            axis=0,
        )

    def box_tile(value):
        a, b, c, d = (value[8 * n : 8 * n + 8] for n in range(4))
        return jnp.where(low, a, d) + swap_halves(jnp.where(low, b, c))

    half = BLOCK // PIECES

    def far_part(h, rows_from, couple_from, far_from, groups, boxes):
        totals = [None] * boxes
        lane_slot = lax.broadcasted_iota(jnp.int32, (32, 512), 1) % GROUP
        for g in range(groups):
            left = turned(gathered[pl.ds(rows_from + GROUP * g, GROUP), :])
            right = stacked(
                couples[pl.ds(couple_from + GROUP * g, GROUP), h * half : (h + 1) * half]
            )
            touched = [
                b
                for b in range(boxes)
                if b * LIST < GROUP * (g + 1) and (b + 1) * LIST > GROUP * g
            ]
            if len(touched) == 2:
                border = touched[1] * LIST - GROUP * g
                zero = jnp.zeros_like(left)
                left = jnp.concatenate(
                    [
                        jnp.where(lane_slot < border, left, zero),
                        jnp.where(lane_slot < border, zero, left),
                    ],
                    axis=0,
                )
            value = jnp.dot(left, right, preferred_element_type=F32)
            for n, b in enumerate(touched):
                part = value[32 * n : 32 * n + 32]
                totals[b] = part if totals[b] is None else totals[b] + part
        for b in range(boxes):
            rows = pl.ds(far_from + 8 * b, 8)
            if h == 0:
                far[rows, :] = box_tile(totals[b])
            else:
                far[rows, :] += box_tile(totals[b])

    def gather_0(h):
        sources = win_a[h].reshape(WINDOW * 64, PART)

        def step(n, carry):
            rows = pl.ds(pl.multiple_of(n * 896, 896), 896)
            gathered[rows, :] = jnp.dot(
                hot_0[rows, :], sources, preferred_element_type=F32
            ).astype(BF16)
            return carry

        lax.fori_loop(0, 2, step, 0)

    def far_0(h, first, last):
        def step(n, carry):
            row = pl.multiple_of(n * WIDE, WIDE)
            far_part(h, row, row, pl.multiple_of(n * 64, 64), 7, 8)
            return carry

        lax.fori_loop(first, last, step, 0, unroll=2)

    arrived_direct(win_a.at[0], recv_a.at[0])
    shared = shared_rows(win_a.at[0], pass_a.at[0], recv_a.at[0])
    start(shared)
    all_sends += shared
    copies[6].wait()
    pad3[...] = jnp.zeros_like(pad3)
    pad3[0:28, :] = c3[...].astype(F32)
    couples[2352:2384, :] = pad3[...].astype(BF16)
    couples[2384:2400, :] = jnp.zeros((16, BLOCK), BF16)
    arrived_passed(win_a.at[0], recv_a.at[0])
    gather_0(0)
    copies[8].wait()
    far_0(0, 0, 4)
    arrived_direct(win_a.at[1], recv_a.at[1])
    shared = shared_rows(win_a.at[1], pass_a.at[1], recv_a.at[1])
    start(shared)
    all_sends += shared
    for k in range(1, rows):
        pltpu.make_async_copy(top.at[y, z], top.at[y, z], recv_z.at[k]).wait()
    sends_y = [
        whole(top.at[y], along_y(k), send_y.at[k], recv_y.at[planes - k])
        for k in range(1, planes)
    ]
    for copy in sends_y:
        copy.start()
    back = member + 1 - 2 * lax.rem(member, 2)
    pltpu.make_async_copy(c4.at[back], c4.at[back], recv_c.at[0]).wait()
    sends_c.append(whole(c4.at[back], sibling, send_c.at[2], recv_c.at[2]))
    sends_c[2].start()
    far_0(0, 4, 8)

    arrived_passed(win_a.at[1], recv_a.at[1])
    gather_0(1)
    far_0(1, 0, 4)
    arrived_direct(win_b, recv_b)
    shared = shared_rows(win_b, pass_b, recv_b)
    start(shared)
    all_sends += shared
    far_0(1, 4, 8)

    arrived_passed(win_b, recv_b)
    copies[9].wait()
    copies[10].wait()
    for h in range(PIECES):
        gathered[0:608, :] = jnp.dot(
            hot_1[...],
            win_b[:, :, h * PART : (h + 1) * PART].reshape(WINDOW * 32, PART),
            preferred_element_type=F32,
        ).astype(BF16)

        def far_1(n, carry):
            row = pl.multiple_of(n * WIDE, WIDE)
            far_part(h, row, 1792 + row, 512 + pl.multiple_of(n * 64, 64), 7, 8)
            return carry

        lax.fori_loop(0, 2, far_1, 0)
        far_part(h, 448, 2240, 640, 5, 5)

    for k in range(1, planes):
        pltpu.make_async_copy(top.at[y], top.at[y], recv_y.at[k]).wait()
    for v in (1, 2, 3):
        pltpu.make_async_copy(slots_4.at[0], slots_4.at[0], recv_s.at[v]).wait()
    for v in (1, 2):
        pltpu.make_async_copy(c4.at[0], c4.at[0], recv_c.at[v]).wait()
    pad4[...] = jnp.zeros_like(pad4)
    for n in range(4):
        pad4[7 * n : 7 * n + 7, :] = c4[n].astype(F32)
        lines[n : n + 1, :] = slots_4[n, 0:1, :]
    columns = lines[...].T
    for n in range(4):
        index[2560 + 7 * n : 2568 + 7 * n, :] = jnp.broadcast_to(columns[:8, n : n + 1], (8, LANES))
    few = lax.broadcasted_iota(jnp.int32, (32, LANES), 0)
    index[2560:2592, :] = jnp.where(few < counts_4[group], index[2560:2592, :], -1)
    tops = 2 * rows * planes
    count = max(tops, 8)
    if tops < 8:
        tiles[0:512, :] = jnp.zeros((512, LANES), F32)
    for box in range(tops):
        tiles[pl.ds((box // 8) * 64 + box % 8, 8, stride=8), :] = top[
            box // 2 // rows, box // 2 % rows, box % 2
        ]
    natural = jnp.concatenate(
        [
            jnp.concatenate(
                [tiles[(big * 8 + j) * 8 : (big * 8 + j) * 8 + 8, :] for j in range(8)], axis=1
            )
            for big in range(count // 8)
        ],
        axis=0,
    ).astype(BF16)
    top_rows = jnp.dot(natural, perm[...], preferred_element_type=F32).astype(BF16)
    rows_4 = jnp.dot(one_hot(2560, 32, count), top_rows, preferred_element_type=F32).astype(BF16)
    blocks_4 = pad4[...].astype(BF16)
    far_4 = box_tile(
        sum(
            jnp.dot(
                turned(rows_4[:, h * PART : (h + 1) * PART]),
                stacked(blocks_4[:, h * half : (h + 1) * half]),
                preferred_element_type=F32,
            )
            for h in range(PIECES)
        )
    )

    def lowered(parent, n, boxes):
        rows = jnp.concatenate(
            [jnp.where(low, parent, 0.0), jnp.where(low, swap_halves(parent), 0.0)], axis=0
        ).astype(BF16)
        product = lax.dot_general(
            rows,
            up_b[n * 256 : n * 256 + boxes * RANK, :],
            (((1,), (1,)), ((), ())),
            preferred_element_type=F32,
        )
        result = []
        for pair in range(0, boxes, 2):
            even = product[:8, pair * RANK : pair * RANK + LANES]
            odd = product[8:, pair * RANK : pair * RANK + LANES]
            result.append(jnp.where(low, even, swap_halves(odd)))
            result.append(jnp.where(low, swap_halves(even), odd))
        return result

    field_3 = far[672:680, :] + lowered(far_4, 21, 2)[0]
    down = lowered(field_3, 20, 4)
    field_2 = [far[640 + 8 * c : 648 + 8 * c, :] + down[c] for c in range(4)]
    field_1 = []
    for p in range(4):
        down = lowered(field_2[p], 16 + p, 4)
        for c in range(4):
            row = 512 + 8 * (4 * p + c)
            field_1.append(far[row : row + 8, :] + down[c])
    for p in range(16):
        down = lowered(field_1[p], p, 4)
        for c in range(4):
            box = 4 * p + c
            tiles[pl.ds((box // 8) * 64 + box % 8, 8, stride=8), :] = (
                far[8 * box : 8 * box + 8, :] + down[c]
            )
    for big in range(8):
        for j in range(8):
            row = (big * 8 + j) * 8
            out[big * 8 : big * 8 + 8, j * LANES : (j + 1) * LANES] = tiles[row : row + 8, :]

    for copy in sends_t + sends_s + sends_c + sends_z + sends_y:
        copy.wait_send()
    sent(all_sends)


def solution(mesh):
    devices = mesh.shape["wide"] * mesh.shape["narrow"]
    planes = max(1, devices // 32)
    split = P(("wide", "narrow"), None)
    line = P(("wide", "narrow"))
    anywhere = pl.BlockSpec(memory_space=pl.ANY)
    scalars = pl.BlockSpec(memory_space=pltpu.SMEM)
    inside = pl.BlockSpec(memory_space=pltpu.VMEM)
    vmem = pltpu.VMEM
    dma = pltpu.SemaphoreType.DMA

    def body(*arrays):
        return pl.pallas_call(
            functools.partial(kernel, devices, planes),
            out_shape=jax.ShapeDtypeStruct((64, WIDTH), F32),
            in_specs=[anywhere] * 11 + [inside] * 4 + [scalars] * 5,
            out_specs=pl.BlockSpec(memory_space=pltpu.VMEM),
            scratch_shapes=[
                vmem((64, WIDTH), F32),
                vmem((64, BLOCK), BF16),
                vmem((16, BLOCK), BF16),
                vmem((4, BLOCK), BF16),
                vmem((1, BLOCK), BF16),
                vmem((2400, BLOCK), BF16),
                vmem((28, BLOCK), BF16),
                vmem((4, 7, BLOCK), BF16),
                vmem((1792,), jnp.int32),
                vmem((32, BLOCK), F32),
                vmem((32, BLOCK), F32),
                vmem((512, LANES), F32),
                vmem((256, LANES), F32),
                vmem((WIDTH, WIDTH), BF16),
                vmem((PIECES, WINDOW, 64, PART), BF16),
                vmem((WINDOW, 32, WIDTH), BF16),
                vmem((16, BLOCK), F32),
                vmem((512, 512), BF16),
                vmem((256, 256), BF16),
                vmem((96 * RANK, LANES), BF16),
                vmem((32, LANES), jnp.int32),
                vmem((21 * LANES, LANES), jnp.int32),
                vmem((1792, WINDOW * 64), BF16),
                vmem((608, WINDOW * 32), BF16),
                vmem((1792, PART), BF16),
                vmem((85 * 8, LANES), F32),
                vmem((8, 8, LANES), F32),
                vmem((planes, devices // 8 // planes, 2, 8, LANES), F32),
                vmem((4, 8, LANES), jnp.int32),
                dma((11,)),
                dma((PIECES, 2 * REACH)),
                dma((PIECES, WINDOW)),
                dma((PIECES, WINDOW)),
                dma((2 * REACH,)),
                dma((WINDOW,)),
                dma((WINDOW,)),
                dma((8,)),
                dma((8,)),
                dma((4,)),
                dma((4,)),
                dma((4,)),
                dma((4,)),
                dma((4,)),
                dma((4,)),
                dma((3,)),
                dma((3,)),
            ],
            compiler_params=pltpu.CompilerParams(
                collective_id=0, has_side_effects=True, vmem_limit_bytes=56 * 1024 * 1024
            ),
        )(*arrays)

    return jax.shard_map(
        body,
        mesh=mesh,
        in_specs=(split,) * 10 + (line,) * 9 + (P(),),
        out_specs=split,
        check_vma=False,
    )
```

```python
import functools

import jax
import jax.numpy as jnp
from jax import lax
from jax.experimental import pallas as pl
from jax.experimental.pallas import tpu as pltpu
from jax.sharding import PartitionSpec as P

RANK = 64
RHS = 16
LIST = 28
REACH = 4
WIDTH = RHS * RANK
BLOCK = RANK * RANK
LANES = 128
SUPER = 4 * LIST
GROUP = 32
WIDE = 2 * SUPER
PIECES = 2
PART = WIDTH // PIECES
WINDOW = 2 * REACH + 1
MESH = pl.DeviceIdType.MESH
BF16 = jnp.bfloat16
F32 = jnp.float32


def low_lanes(shape):
    return lax.broadcasted_iota(jnp.int32, shape, 1) < RANK


def swap_halves(value):
    return pltpu.roll(value, RANK, 1)


def kernel(
    devices,
    planes,
    moments,
    up_0,
    up_1,
    up_2,
    up_3,
    couple_0,
    couple_1,
    couple_2,
    couple_3,
    couple_4,
    sources_0,
    sources_1,
    sources_2,
    sources_3,
    sources_4,
    counts_0,
    counts_1,
    counts_2,
    counts_3,
    counts_4,
    out,
    mom,
    u0,
    u1,
    u2,
    u3,
    couples,
    c3,
    c4,
    s0,
    pad3,
    pad4,
    tiles,
    rows_b,
    perm,
    win_a,
    win_b,
    few_up,
    by_pair,
    by_row,
    up_b,
    lines,
    index,
    hot_0,
    hot_1,
    gathered,
    far,
    terms,
    top,
    slots_4,
    load_sem,
    send_a,
    recv_a,
    pass_a,
    send_b,
    recv_b,
    pass_b,
    send_t,
    recv_t,
    send_z,
    recv_z,
    send_y,
    recv_y,
    send_s,
    recv_s,
    send_c,
    recv_c,
):
    rows = devices // 8 // planes
    me = lax.axis_index("wide") * 2 + lax.axis_index("narrow")
    member = lax.rem(me, 4)
    group = lax.div(me, 4)
    core = lax.rem(lax.div(me, 2), 2)
    seat = lax.rem(me, 8)
    my_row = lax.div(me, 8)
    z, y = lax.rem(my_row, rows), lax.div(my_row, rows)
    opposite = me + 1 - 2 * lax.rem(me, 2)
    sibling = me + 2 - 4 * core

    def place(position):
        return (lax.div(position, 2), lax.rem(position, 2))

    def mate(v):
        return group * 4 + lax.rem(member + v, 4)

    def row_mate(v):
        return my_row * 8 + lax.rem(seat + v, 8)

    def along_z(k):
        return (y * rows + lax.rem(z + k, rows)) * 8 + seat

    def along_y(k):
        return (lax.rem(y + k, planes) * rows + z) * 8 + seat

    def exists(o):
        return jnp.logical_and(me + o >= 0, me + o < devices)

    offsets = [-4, 4, -3, 3, -1, 1, -2, 2]

    for o in offsets:

        @pl.when(jnp.logical_not(exists(o)))
        def _():
            for h in range(PIECES):
                win_a[h, REACH + o] = jnp.zeros((64, PART), BF16)
            win_b[REACH + o] = jnp.zeros((32, WIDTH), BF16)

    barrier = pltpu.get_barrier_semaphore()

    def greet(position):
        pl.semaphore_signal(barrier, inc=1, device_id=place(position), device_id_type=MESH)

    greeted = jnp.int32(rows - 1 + planes - 1)
    for o in offsets + [-7, -6, -5, 5, 6, 7]:
        known = exists(o)
        if abs(o) > REACH:
            known = jnp.logical_and(seat + o >= 0, seat + o < 8)
        pl.when(known)(functools.partial(greet, me + o))
        greeted = greeted + known.astype(jnp.int32)
    for k in range(1, rows):
        greet(along_z(k))
    for k in range(1, planes):
        greet(along_y(k))

    loads = [
        (moments, mom),
        (up_0, u0),
        (up_1, u1),
        (up_2, u2),
        (up_3, u3),
        (sources_0, s0),
        (couple_3, c3),
        (couple_4, c4.at[member]),
        (couple_0, couples.at[pl.ds(0, 1792)]),
        (couple_1, couples.at[pl.ds(1792, 448)]),
        (couple_2, couples.at[pl.ds(2240, 112)]),
    ]
    copies = [
        pltpu.make_async_copy(src, dst, load_sem.at[n]) for n, (src, dst) in enumerate(loads)
    ]
    for copy in copies:
        copy.start()

    natural_lane = lax.broadcasted_iota(jnp.int32, (LANES, LANES), 0)
    wanted = (natural_lane & (RANK - 1)) * RHS + (natural_lane >> 6) * 8
    ahead = wanted - lax.broadcasted_iota(jnp.int32, (LANES, LANES), 1)

    def build_perm(j, carry):
        first_row = pl.multiple_of(j * LANES, LANES)
        for n in range(WIDTH // LANES):
            perm[pl.ds(first_row, LANES), n * LANES : (n + 1) * LANES] = jnp.where(
                ahead == n * LANES - j, 1.0, 0.0
            ).astype(BF16)
        return carry

    lax.fori_loop(0, 8, build_perm, 0)
    copies[0].wait()
    own = jnp.dot(mom[...].astype(BF16), perm[...], preferred_element_type=F32).astype(BF16)
    for h in range(PIECES):
        win_a[h, REACH] = own[:, h * PART : (h + 1) * PART]

    pl.semaphore_wait(barrier, greeted)

    def when(condition, act):
        pl.when(condition)(act)

    def direct(window, send, recv):
        result = []
        for n, o in enumerate(offsets):
            target = me + o
            target_core = lax.rem(lax.div(target + 4, 2), 2)
            condition = exists(o)
            if o != -1:
                condition = jnp.logical_and(condition, target_core == (0 if o > 0 else 1))
            copy = pltpu.make_async_remote_copy(
                src_ref=window.at[REACH],
                dst_ref=window.at[REACH - o],
                send_sem=send.at[n],
                recv_sem=recv.at[REACH - o],
                device_id=place(target),
                device_id_type=MESH,
            )
            result.append((condition, copy))
        return result

    def passes(window, send, recv, slots):
        result = []
        for which, by in ((0, -2), (1, 2)):
            for slot in slots[which]:
                copy = pltpu.make_async_remote_copy(
                    src_ref=window.at[slot],
                    dst_ref=window.at[slot + by],
                    send_sem=send.at[slot],
                    recv_sem=recv.at[slot + by],
                    device_id=place(me - by),
                    device_id_type=MESH,
                )
                result.append((jnp.logical_and(core == which, exists(slot - REACH)), copy))
        return result

    def own_rows(window, send, recv):
        return passes(window, send, recv, ([REACH], [REACH]))

    def shared_rows(window, send, recv):
        return passes(window, send, recv, ([2, 3, 5], [5, 6]))

    def start(copies):
        for condition, copy in copies:
            when(condition, copy.start)

    def sent(copies):
        for condition, copy in copies:
            when(condition, copy.wait_send)

    def arrived(window, recv, slots):
        for which in (0, 1):
            for slot in slots[which]:
                copy = pltpu.make_async_copy(window.at[slot], window.at[slot], recv.at[slot])
                when(jnp.logical_and(core == which, exists(slot - REACH)), copy.wait)

    def arrived_direct(window, recv):
        arrived(window, recv, ([0, 1, 2, 3, 5], [5, 6, 7, 8]))

    def arrived_passed(window, recv):
        arrived(window, recv, ([6, 7, 8], [0, 1, 2, 3]))

    def send_part(h):
        result = direct(win_a.at[h], send_a.at[h], recv_a.at[h])
        result += own_rows(win_a.at[h], pass_a.at[h], recv_a.at[h])
        start(result)
        return result

    all_sends = send_part(0)

    def whole(ref, to, send_sem, recv_sem):
        return pltpu.make_async_remote_copy(
            src_ref=ref,
            dst_ref=ref,
            send_sem=send_sem,
            recv_sem=recv_sem,
            device_id=place(to),
            device_id_type=MESH,
        )

    a = lax.broadcasted_iota(jnp.int32, (512, 512), 0)
    b = lax.broadcasted_iota(jnp.int32, (512, 512), 1)
    by_pair[...] = jnp.where(b == (a & 31) * 16 + (a >> 5), 1.0, 0.0).astype(BF16)
    a = lax.broadcasted_iota(jnp.int32, (256, 256), 0)
    b = lax.broadcasted_iota(jnp.int32, (256, 256), 1)
    by_row[...] = jnp.where(b == (a & 1) * 128 + (a >> 1), 1.0, 0.0).astype(BF16)

    for n in range(1, 5):
        copies[n].wait()
    few_up[...] = jnp.zeros_like(few_up)
    few_up[0:4, :] = u2[...].astype(F32)
    few_up[4:5, :] = u3[...].astype(F32)
    blocks = [u0[16 * n : 16 * n + 16, :] for n in range(4)]
    blocks += [u1[...], few_up[...].astype(BF16)]
    columns = jnp.concatenate(
        [
            jnp.concatenate([block[:, m * LANES : (m + 1) * LANES] for m in range(32)], axis=0)
            for block in blocks
        ],
        axis=1,
    )
    by_box = jnp.dot(by_pair[...], columns, preferred_element_type=F32)
    for n in range(6):
        quads = []
        for p in range(4 if n < 5 else 2):
            one = by_box[128 * p : 128 * p + 128, n * LANES : (n + 1) * LANES]
            quads.append(jnp.concatenate([one, swap_halves(one)], axis=0).astype(BF16))
        upright = jnp.dot(
            by_row[...], jnp.concatenate(quads, axis=1), preferred_element_type=F32
        ).astype(BF16)
        for p in range(len(quads)):
            base = (4 * n + p) * 256
            up_b[base : base + 256, :] = upright[:, p * LANES : (p + 1) * LANES]

    for big in range(8):
        for j in range(8):
            tiles[pl.ds((big * 8 + j) * 8, 8), :] = mom[
                big * 8 : big * 8 + 8, j * LANES : (j + 1) * LANES
            ]

    low = low_lanes((8, LANES))

    def beside(first, second):
        even = jnp.where(low, first, swap_halves(second))
        odd = jnp.where(low, swap_halves(first), second)
        return jnp.concatenate([even, odd], axis=0)

    def lifted(children, base):
        left = beside(children[0], children[1])
        right = beside(children[2], children[3])
        rows = jnp.concatenate([left, right], axis=1).astype(BF16)
        product = jnp.dot(
            rows, up_b[base * RANK : (base + 4) * RANK, :], preferred_element_type=F32
        )
        return jnp.where(low, product[:8], swap_halves(product[8:]))

    def tile_of(box):
        return tiles[pl.ds((box // 8) * 64 + box % 8, 8, stride=8), :]

    level_1 = [lifted([tile_of(4 * p + c) for c in range(4)], 4 * p) for p in range(16)]
    level_2 = [lifted(level_1[4 * p : 4 * p + 4], 64 + 4 * p) for p in range(4)]
    level_3 = lifted(level_2, 80)
    alone = jnp.concatenate([level_3, swap_halves(level_3)], axis=0)[:, :RANK].astype(BF16)
    product = jnp.dot(alone, up_b[84 * RANK : 85 * RANK, :], preferred_element_type=F32)
    terms[seat] = jnp.where(low, product[:8], swap_halves(product[8:]))

    sends_t = [
        whole(terms.at[seat], row_mate(v), send_t.at[v], recv_t.at[8 - v]) for v in range(1, 8)
    ]
    for copy in sends_t:
        copy.start()

    all_sends += send_part(1)

    rows_b[...] = jnp.zeros_like(rows_b)
    for row, value in enumerate(level_1 + level_2 + [level_3]):
        rows_b[pl.ds((row // 8) * 64 + row % 8, 8, stride=8), :] = value
    natural = jnp.concatenate(
        [
            jnp.concatenate(
                [rows_b[(big * 8 + j) * 8 : (big * 8 + j) * 8 + 8, :] for j in range(8)], axis=1
            )
            for big in range(4)
        ],
        axis=0,
    ).astype(BF16)
    win_b[REACH] = jnp.dot(natural, perm[...], preferred_element_type=F32).astype(BF16)

    copies[5].wait()
    first = me - REACH
    for j in range(14):
        lines[j : j + 1, :] = s0[pl.ds(j * LANES, LANES)].reshape(1, LANES) - first * 64
    lines[14:32, :] = jnp.zeros((18, LANES), jnp.int32)
    for j in range(4):
        length = min(LANES, 448 - j * LANES)
        local = sources_1[pl.ds(j * LANES, length)].reshape(1, length) - first * 16
        lines[14 + j : 15 + j, :length] = (local >> 4) * 32 + (local & 15)
    local = sources_2[...].reshape(1, 112) - first * 4
    lines[18:19, :112] = (local >> 2) * 32 + 16 + (local & 3)
    lines[19:20, :28] = (sources_3[...].reshape(1, 28) - first) * 32 + 20
    columns = lines[...].T
    places = [j * LANES for j in range(18)] + [2240, 2352]
    for j, row in enumerate(places):
        index[row : row + LANES, :] = jnp.broadcast_to(columns[:, j : j + 1], (LANES, LANES))

    slot = lax.broadcasted_iota(jnp.int32, (SUPER, LANES), 0)

    def drop_invalid(base, counts):
        limit = counts[3] + 3 * LIST
        for b in (2, 1, 0):
            limit = jnp.where(slot < (b + 1) * LIST, counts[b] + b * LIST, limit)
        rows = pl.ds(base, SUPER)
        index[rows, :] = jnp.where(slot < limit, index[rows, :], -1)

    def drop_level(first_row, counts_ref, n):
        def step(n, carry):
            base = pl.multiple_of(first_row + n * SUPER, 16)
            drop_invalid(base, [counts_ref[4 * n + b] for b in range(4)])
            return carry

        lax.fori_loop(0, n, step, 0)

    drop_level(0, counts_0, 16)
    drop_level(1792, counts_1, 4)
    drop_level(2240, counts_2, 1)
    few = lax.broadcasted_iota(jnp.int32, (48, LANES), 0)
    index[2352:2400, :] = jnp.where(few < counts_3[0], index[2352:2400, :], -1)

    def one_hot(from_row, count, width):
        place_of = index[pl.ds(from_row, count), :]
        lane = lax.broadcasted_iota(jnp.int32, (count, LANES), 1)
        hot = [
            jnp.where(place_of == lane + first_lane, 1.0, 0.0).astype(BF16)[
                :, : min(LANES, width - first_lane)
            ]
            for first_lane in range(0, width, LANES)
        ]
        return jnp.concatenate(hot, axis=1) if len(hot) > 1 else hot[0]

    def mark_0(n, carry):
        row = pl.multiple_of(n * LANES, LANES)
        hot_0[pl.ds(row, LANES), :] = one_hot(row, LANES, WINDOW * 64)
        return carry

    lax.fori_loop(0, 14, mark_0, 0)

    def mark_1(n, carry):
        row = pl.multiple_of(n * 304, 16)
        hot_1[pl.ds(row, 304), :] = one_hot(pl.multiple_of(1792 + row, 16), 304, WINDOW * 32)
        return carry

    lax.fori_loop(0, 2, mark_1, 0)

    for v in range(1, 8):
        pltpu.make_async_copy(terms.at[0], terms.at[0], recv_t.at[v]).wait()
    for n in range(2):
        four = [terms[4 * n + c] for c in range(4)]
        top[y, z, n] = (four[0] + four[1]) + (four[2] + four[3])
    sends_z = [
        whole(top.at[y, z], along_z(k), send_z.at[k], recv_z.at[rows - k])
        for k in range(1, rows)
    ]
    for copy in sends_z:
        copy.start()
    slots_4[member] = jnp.zeros((8, LANES), jnp.int32)
    slots_4[member, 0:1, :7] = sources_4[...].reshape(1, 7)
    copies[7].wait()
    sends_s = [
        whole(slots_4.at[member], mate(v), send_s.at[v], recv_s.at[4 - v]) for v in (1, 2, 3)
    ]
    sends_c = [
        whole(c4.at[member], opposite, send_c.at[0], recv_c.at[0]),
        whole(c4.at[member], sibling, send_c.at[1], recv_c.at[1]),
    ]
    for copy in sends_s + sends_c:
        copy.start()


    for copies_b in (direct(win_b, send_b, recv_b), own_rows(win_b, pass_b, recv_b)):
        start(copies_b)
        all_sends += copies_b

    def turned(rows):
        stack = jnp.concatenate(
            [rows[:, i * LANES : (i + 1) * LANES] for i in range(4)], axis=0
        )
        across = stack.T
        return jnp.concatenate([across[32 * m : 32 * m + 32] for m in range(4)], axis=1)

    def stacked(rows):
        return jnp.concatenate(
            [
                rows[:, (4 * i + m) * LANES : (4 * i + m + 1) * LANES]
                for m in range(4)
                for i in range(4)
            ],
            axis=0,
        )

    def box_tile(value):
        a, b, c, d = (value[8 * n : 8 * n + 8] for n in range(4))
        return jnp.where(low, a, d) + swap_halves(jnp.where(low, b, c))

    half = BLOCK // PIECES

    def far_part(h, rows_from, couple_from, far_from, groups, boxes):
        totals = [None] * boxes
        lane_slot = lax.broadcasted_iota(jnp.int32, (32, 512), 1) % GROUP
        for g in range(groups):
            left = turned(gathered[pl.ds(rows_from + GROUP * g, GROUP), :])
            right = stacked(
                couples[pl.ds(couple_from + GROUP * g, GROUP), h * half : (h + 1) * half]
            )
            touched = [
                b
                for b in range(boxes)
                if b * LIST < GROUP * (g + 1) and (b + 1) * LIST > GROUP * g
            ]
            if len(touched) == 2:
                border = touched[1] * LIST - GROUP * g
                zero = jnp.zeros_like(left)
                left = jnp.concatenate(
                    [
                        jnp.where(lane_slot < border, left, zero),
                        jnp.where(lane_slot < border, zero, left),
                    ],
                    axis=0,
                )
            value = jnp.dot(left, right, preferred_element_type=F32)
            for n, b in enumerate(touched):
                part = value[32 * n : 32 * n + 32]
                totals[b] = part if totals[b] is None else totals[b] + part
        for b in range(boxes):
            rows = pl.ds(far_from + 8 * b, 8)
            if h == 0:
                far[rows, :] = box_tile(totals[b])
            else:
                far[rows, :] += box_tile(totals[b])

    def gather_0(h):
        sources = win_a[h].reshape(WINDOW * 64, PART)

        def step(n, carry):
            rows = pl.ds(pl.multiple_of(n * 896, 896), 896)
            gathered[rows, :] = jnp.dot(
                hot_0[rows, :], sources, preferred_element_type=F32
            ).astype(BF16)
            return carry

        lax.fori_loop(0, 2, step, 0)

    def far_0(h, first, last):
        def step(n, carry):
            row = pl.multiple_of(n * WIDE, WIDE)
            far_part(h, row, row, pl.multiple_of(n * 64, 64), 7, 8)
            return carry

        lax.fori_loop(first, last, step, 0, unroll=2)

    arrived_direct(win_a.at[0], recv_a.at[0])
    shared = shared_rows(win_a.at[0], pass_a.at[0], recv_a.at[0])
    start(shared)
    all_sends += shared
    copies[6].wait()
    pad3[...] = jnp.zeros_like(pad3)
    pad3[0:28, :] = c3[...].astype(F32)
    couples[2352:2384, :] = pad3[...].astype(BF16)
    couples[2384:2400, :] = jnp.zeros((16, BLOCK), BF16)
    arrived_passed(win_a.at[0], recv_a.at[0])
    gather_0(0)
    copies[8].wait()
    far_0(0, 0, 4)
    arrived_direct(win_a.at[1], recv_a.at[1])
    shared = shared_rows(win_a.at[1], pass_a.at[1], recv_a.at[1])
    start(shared)
    all_sends += shared
    for k in range(1, rows):
        pltpu.make_async_copy(top.at[y, z], top.at[y, z], recv_z.at[k]).wait()
    sends_y = [
        whole(top.at[y], along_y(k), send_y.at[k], recv_y.at[planes - k])
        for k in range(1, planes)
    ]
    for copy in sends_y:
        copy.start()
    back = member + 1 - 2 * lax.rem(member, 2)
    pltpu.make_async_copy(c4.at[back], c4.at[back], recv_c.at[0]).wait()
    sends_c.append(whole(c4.at[back], sibling, send_c.at[2], recv_c.at[2]))
    sends_c[2].start()
    far_0(0, 4, 8)

    arrived_passed(win_a.at[1], recv_a.at[1])
    gather_0(1)
    far_0(1, 0, 4)
    arrived_direct(win_b, recv_b)
    shared = shared_rows(win_b, pass_b, recv_b)
    start(shared)
    all_sends += shared
    far_0(1, 4, 8)

    for k in range(1, planes):
        pltpu.make_async_copy(top.at[y], top.at[y], recv_y.at[k]).wait()
    for v in (1, 2, 3):
        pltpu.make_async_copy(slots_4.at[0], slots_4.at[0], recv_s.at[v]).wait()
    for v in (1, 2):
        pltpu.make_async_copy(c4.at[0], c4.at[0], recv_c.at[v]).wait()
    pad4[...] = jnp.zeros_like(pad4)
    for n in range(4):
        pad4[7 * n : 7 * n + 7, :] = c4[n].astype(F32)
        lines[n : n + 1, :] = slots_4[n, 0:1, :]
    columns = lines[...].T
    for n in range(4):
        index[2560 + 7 * n : 2568 + 7 * n, :] = jnp.broadcast_to(columns[:8, n : n + 1], (8, LANES))
    few = lax.broadcasted_iota(jnp.int32, (32, LANES), 0)
    index[2560:2592, :] = jnp.where(few < counts_4[group], index[2560:2592, :], -1)
    tops = 2 * rows * planes
    count = max(tops, 8)
    if tops < 8:
        tiles[0:512, :] = jnp.zeros((512, LANES), F32)
    for box in range(tops):
        tiles[pl.ds((box // 8) * 64 + box % 8, 8, stride=8), :] = top[
            box // 2 // rows, box // 2 % rows, box % 2
        ]
    natural = jnp.concatenate(
        [
            jnp.concatenate(
                [tiles[(big * 8 + j) * 8 : (big * 8 + j) * 8 + 8, :] for j in range(8)], axis=1
            )
            for big in range(count // 8)
        ],
        axis=0,
    ).astype(BF16)
    top_rows = jnp.dot(natural, perm[...], preferred_element_type=F32).astype(BF16)
    rows_4 = jnp.dot(one_hot(2560, 32, count), top_rows, preferred_element_type=F32).astype(BF16)
    blocks_4 = pad4[...].astype(BF16)
    far_4 = box_tile(
        sum(
            jnp.dot(
                turned(rows_4[:, h * PART : (h + 1) * PART]),
                stacked(blocks_4[:, h * half : (h + 1) * half]),
                preferred_element_type=F32,
            )
            for h in range(PIECES)
        )
    )

    arrived_passed(win_b, recv_b)
    copies[9].wait()
    copies[10].wait()
    for h in range(PIECES):
        gathered[0:608, :] = jnp.dot(
            hot_1[...],
            win_b[:, :, h * PART : (h + 1) * PART].reshape(WINDOW * 32, PART),
            preferred_element_type=F32,
        ).astype(BF16)

        def far_1(n, carry):
            row = pl.multiple_of(n * WIDE, WIDE)
            far_part(h, row, 1792 + row, 512 + pl.multiple_of(n * 64, 64), 7, 8)
            return carry

        lax.fori_loop(0, 2, far_1, 0)
        far_part(h, 448, 2240, 640, 5, 5)

    def lowered(parent, n, boxes):
        rows = jnp.concatenate(
            [jnp.where(low, parent, 0.0), jnp.where(low, swap_halves(parent), 0.0)], axis=0
        ).astype(BF16)
        product = lax.dot_general(
            rows,
            up_b[n * 256 : n * 256 + boxes * RANK, :],
            (((1,), (1,)), ((), ())),
            preferred_element_type=F32,
        )
        result = []
        for pair in range(0, boxes, 2):
            even = product[:8, pair * RANK : pair * RANK + LANES]
            odd = product[8:, pair * RANK : pair * RANK + LANES]
            result.append(jnp.where(low, even, swap_halves(odd)))
            result.append(jnp.where(low, swap_halves(even), odd))
        return result

    field_3 = far[672:680, :] + lowered(far_4, 21, 2)[0]
    down = lowered(field_3, 20, 4)
    field_2 = [far[640 + 8 * c : 648 + 8 * c, :] + down[c] for c in range(4)]
    field_1 = []
    for p in range(4):
        down = lowered(field_2[p], 16 + p, 4)
        for c in range(4):
            row = 512 + 8 * (4 * p + c)
            field_1.append(far[row : row + 8, :] + down[c])
    for p in range(16):
        down = lowered(field_1[p], p, 4)
        for c in range(4):
            box = 4 * p + c
            tiles[pl.ds((box // 8) * 64 + box % 8, 8, stride=8), :] = (
                far[8 * box : 8 * box + 8, :] + down[c]
            )
    for big in range(8):
        for j in range(8):
            row = (big * 8 + j) * 8
            out[big * 8 : big * 8 + 8, j * LANES : (j + 1) * LANES] = tiles[row : row + 8, :]

    for copy in sends_t + sends_s + sends_c + sends_z + sends_y:
        copy.wait_send()
    sent(all_sends)


def solution(mesh):
    devices = mesh.shape["wide"] * mesh.shape["narrow"]
    planes = max(1, devices // 32)
    split = P(("wide", "narrow"), None)
    line = P(("wide", "narrow"))
    anywhere = pl.BlockSpec(memory_space=pl.ANY)
    scalars = pl.BlockSpec(memory_space=pltpu.SMEM)
    inside = pl.BlockSpec(memory_space=pltpu.VMEM)
    vmem = pltpu.VMEM
    dma = pltpu.SemaphoreType.DMA

    def body(*arrays):
        return pl.pallas_call(
            functools.partial(kernel, devices, planes),
            out_shape=jax.ShapeDtypeStruct((64, WIDTH), F32),
            in_specs=[anywhere] * 11 + [inside] * 4 + [scalars] * 5,
            out_specs=pl.BlockSpec(memory_space=pltpu.VMEM),
            scratch_shapes=[
                vmem((64, WIDTH), F32),
                vmem((64, BLOCK), BF16),
                vmem((16, BLOCK), BF16),
                vmem((4, BLOCK), BF16),
                vmem((1, BLOCK), BF16),
                vmem((2400, BLOCK), BF16),
                vmem((28, BLOCK), BF16),
                vmem((4, 7, BLOCK), BF16),
                vmem((1792,), jnp.int32),
                vmem((32, BLOCK), F32),
                vmem((32, BLOCK), F32),
                vmem((512, LANES), F32),
                vmem((256, LANES), F32),
                vmem((WIDTH, WIDTH), BF16),
                vmem((PIECES, WINDOW, 64, PART), BF16),
                vmem((WINDOW, 32, WIDTH), BF16),
                vmem((16, BLOCK), F32),
                vmem((512, 512), BF16),
                vmem((256, 256), BF16),
                vmem((96 * RANK, LANES), BF16),
                vmem((32, LANES), jnp.int32),
                vmem((21 * LANES, LANES), jnp.int32),
                vmem((1792, WINDOW * 64), BF16),
                vmem((608, WINDOW * 32), BF16),
                vmem((1792, PART), BF16),
                vmem((85 * 8, LANES), F32),
                vmem((8, 8, LANES), F32),
                vmem((planes, devices // 8 // planes, 2, 8, LANES), F32),
                vmem((4, 8, LANES), jnp.int32),
                dma((11,)),
                dma((PIECES, 2 * REACH)),
                dma((PIECES, WINDOW)),
                dma((PIECES, WINDOW)),
                dma((2 * REACH,)),
                dma((WINDOW,)),
                dma((WINDOW,)),
                dma((8,)),
                dma((8,)),
                dma((4,)),
                dma((4,)),
                dma((4,)),
                dma((4,)),
                dma((4,)),
                dma((4,)),
                dma((3,)),
                dma((3,)),
            ],
            compiler_params=pltpu.CompilerParams(
                collective_id=0, has_side_effects=True, vmem_limit_bytes=56 * 1024 * 1024
            ),
        )(*arrays)

    return jax.shard_map(
        body,
        mesh=mesh,
        in_specs=(split,) * 10 + (line,) * 9 + (P(),),
        out_specs=split,
        check_vma=False,
    )
```

```python
import functools

import jax
import jax.numpy as jnp
from jax import lax
from jax.experimental import pallas as pl
from jax.experimental.pallas import tpu as pltpu
from jax.sharding import PartitionSpec as P

RANK = 64
RHS = 16
LIST = 28
REACH = 4
WIDTH = RHS * RANK
BLOCK = RANK * RANK
LANES = 128
SUPER = 4 * LIST
GROUP = 32
WIDE = 2 * SUPER
PIECES = 2
PART = WIDTH // PIECES
WINDOW = 2 * REACH + 1
MESH = pl.DeviceIdType.MESH
BF16 = jnp.bfloat16
F32 = jnp.float32


def low_lanes(shape):
    return lax.broadcasted_iota(jnp.int32, shape, 1) < RANK


def swap_halves(value):
    return pltpu.roll(value, RANK, 1)


def kernel(
    devices,
    planes,
    moments,
    up_0,
    up_1,
    up_2,
    up_3,
    couple_0,
    couple_1,
    couple_2,
    couple_3,
    couple_4,
    sources_0,
    sources_1,
    sources_2,
    sources_3,
    sources_4,
    counts_0,
    counts_1,
    counts_2,
    counts_3,
    counts_4,
    out,
    mom,
    u0,
    u1,
    u2,
    u3,
    couples,
    c3,
    c4,
    s0,
    pad3,
    pad4,
    tiles,
    rows_b,
    perm,
    win_a,
    win_b,
    few_up,
    by_pair,
    by_row,
    up_b,
    lines,
    index,
    hot_0,
    hot_1,
    gathered,
    far,
    terms,
    top,
    slots_4,
    load_sem,
    send_a,
    recv_a,
    pass_a,
    send_b,
    recv_b,
    pass_b,
    send_t,
    recv_t,
    send_z,
    recv_z,
    send_y,
    recv_y,
    send_s,
    recv_s,
    send_c,
    recv_c,
):
    rows = devices // 8 // planes
    me = lax.axis_index("wide") * 2 + lax.axis_index("narrow")
    member = lax.rem(me, 4)
    group = lax.div(me, 4)
    core = lax.rem(lax.div(me, 2), 2)
    seat = lax.rem(me, 8)
    my_row = lax.div(me, 8)
    z, y = lax.rem(my_row, rows), lax.div(my_row, rows)
    opposite = me + 1 - 2 * lax.rem(me, 2)
    sibling = me + 2 - 4 * core

    def place(position):
        return (lax.div(position, 2), lax.rem(position, 2))

    def mate(v):
        return group * 4 + lax.rem(member + v, 4)

    def row_mate(v):
        return my_row * 8 + lax.rem(seat + v, 8)

    def along_z(k):
        return (y * rows + lax.rem(z + k, rows)) * 8 + seat

    def along_y(k):
        return (lax.rem(y + k, planes) * rows + z) * 8 + seat

    def exists(o):
        return jnp.logical_and(me + o >= 0, me + o < devices)

    offsets = [-4, 4, -3, 3, -1, 1, -2, 2]

    for o in offsets:

        @pl.when(jnp.logical_not(exists(o)))
        def _():
            for h in range(PIECES):
                win_a[h, REACH + o] = jnp.zeros((64, PART), BF16)
            win_b[REACH + o] = jnp.zeros((32, WIDTH), BF16)

    barrier = pltpu.get_barrier_semaphore()

    def greet(position):
        pl.semaphore_signal(barrier, inc=1, device_id=place(position), device_id_type=MESH)

    greeted = jnp.int32(rows - 1 + planes - 1)
    for o in offsets + [-7, -6, -5, 5, 6, 7]:
        known = exists(o)
        if abs(o) > REACH:
            known = jnp.logical_and(seat + o >= 0, seat + o < 8)
        pl.when(known)(functools.partial(greet, me + o))
        greeted = greeted + known.astype(jnp.int32)
    for k in range(1, rows):
        greet(along_z(k))
    for k in range(1, planes):
        greet(along_y(k))

    loads = [
        (moments, mom),
        (up_0, u0),
        (up_1, u1),
        (up_2, u2),
        (up_3, u3),
        (sources_0, s0),
        (couple_3, c3),
        (couple_4, c4.at[member]),
        (couple_0, couples.at[pl.ds(0, 1792)]),
        (couple_1, couples.at[pl.ds(1792, 448)]),
        (couple_2, couples.at[pl.ds(2240, 112)]),
    ]
    copies = [
        pltpu.make_async_copy(src, dst, load_sem.at[n]) for n, (src, dst) in enumerate(loads)
    ]
    for copy in copies:
        copy.start()

    natural_lane = lax.broadcasted_iota(jnp.int32, (LANES, LANES), 0)
    wanted = (natural_lane & (RANK - 1)) * RHS + (natural_lane >> 6) * 8
    ahead = wanted - lax.broadcasted_iota(jnp.int32, (LANES, LANES), 1)

    def build_perm(j, carry):
        first_row = pl.multiple_of(j * LANES, LANES)
        for n in range(WIDTH // LANES):
            perm[pl.ds(first_row, LANES), n * LANES : (n + 1) * LANES] = jnp.where(
                ahead == n * LANES - j, 1.0, 0.0
            ).astype(BF16)
        return carry

    lax.fori_loop(0, 8, build_perm, 0)
    copies[0].wait()
    own = jnp.dot(mom[...].astype(BF16), perm[...], preferred_element_type=F32).astype(BF16)
    for h in range(PIECES):
        win_a[h, REACH] = own[:, h * PART : (h + 1) * PART]

    pl.semaphore_wait(barrier, greeted)

    def when(condition, act):
        pl.when(condition)(act)

    def direct(window, send, recv):
        result = []
        for n, o in enumerate(offsets):
            target = me + o
            target_core = lax.rem(lax.div(target + 4, 2), 2)
            condition = exists(o)
            if o != -1:
                condition = jnp.logical_and(condition, target_core == (0 if o > 0 else 1))
            copy = pltpu.make_async_remote_copy(
                src_ref=window.at[REACH],
                dst_ref=window.at[REACH - o],
                send_sem=send.at[n],
                recv_sem=recv.at[REACH - o],
                device_id=place(target),
                device_id_type=MESH,
            )
            result.append((condition, copy))
        return result

    def passes(window, send, recv, slots):
        result = []
        for which, by in ((0, -2), (1, 2)):
            for slot in slots[which]:
                copy = pltpu.make_async_remote_copy(
                    src_ref=window.at[slot],
                    dst_ref=window.at[slot + by],
                    send_sem=send.at[slot],
                    recv_sem=recv.at[slot + by],
                    device_id=place(me - by),
                    device_id_type=MESH,
                )
                result.append((jnp.logical_and(core == which, exists(slot - REACH)), copy))
        return result

    def own_rows(window, send, recv):
        return passes(window, send, recv, ([REACH], [REACH]))

    def shared_rows(window, send, recv):
        return passes(window, send, recv, ([2, 3, 5], [5, 6]))

    def start(copies):
        for condition, copy in copies:
            when(condition, copy.start)

    def sent(copies):
        for condition, copy in copies:
            when(condition, copy.wait_send)

    def arrived(window, recv, slots):
        for which in (0, 1):
            for slot in slots[which]:
                copy = pltpu.make_async_copy(window.at[slot], window.at[slot], recv.at[slot])
                when(jnp.logical_and(core == which, exists(slot - REACH)), copy.wait)

    def arrived_direct(window, recv):
        arrived(window, recv, ([0, 1, 2, 3, 5], [5, 6, 7, 8]))

    def arrived_passed(window, recv):
        arrived(window, recv, ([6, 7, 8], [0, 1, 2, 3]))

    def send_part(h):
        result = direct(win_a.at[h], send_a.at[h], recv_a.at[h])
        result += own_rows(win_a.at[h], pass_a.at[h], recv_a.at[h])
        start(result)
        return result

    all_sends = send_part(0)

    def whole(ref, to, send_sem, recv_sem):
        return pltpu.make_async_remote_copy(
            src_ref=ref,
            dst_ref=ref,
            send_sem=send_sem,
            recv_sem=recv_sem,
            device_id=place(to),
            device_id_type=MESH,
        )

    a = lax.broadcasted_iota(jnp.int32, (512, 512), 0)
    b = lax.broadcasted_iota(jnp.int32, (512, 512), 1)
    by_pair[...] = jnp.where(b == (a & 31) * 16 + (a >> 5), 1.0, 0.0).astype(BF16)
    a = lax.broadcasted_iota(jnp.int32, (256, 256), 0)
    b = lax.broadcasted_iota(jnp.int32, (256, 256), 1)
    by_row[...] = jnp.where(b == (a & 1) * 128 + (a >> 1), 1.0, 0.0).astype(BF16)

    for n in range(1, 5):
        copies[n].wait()
    few_up[...] = jnp.zeros_like(few_up)
    few_up[0:4, :] = u2[...].astype(F32)
    few_up[4:5, :] = u3[...].astype(F32)
    blocks = [u0[16 * n : 16 * n + 16, :] for n in range(4)]
    blocks += [u1[...], few_up[...].astype(BF16)]
    columns = jnp.concatenate(
        [
            jnp.concatenate([block[:, m * LANES : (m + 1) * LANES] for m in range(32)], axis=0)
            for block in blocks
        ],
        axis=1,
    )
    by_box = jnp.dot(by_pair[...], columns, preferred_element_type=F32)
    for n in range(6):
        quads = []
        for p in range(4 if n < 5 else 2):
            one = by_box[128 * p : 128 * p + 128, n * LANES : (n + 1) * LANES]
            quads.append(jnp.concatenate([one, swap_halves(one)], axis=0).astype(BF16))
        upright = jnp.dot(
            by_row[...], jnp.concatenate(quads, axis=1), preferred_element_type=F32
        ).astype(BF16)
        for p in range(len(quads)):
            base = (4 * n + p) * 256
            up_b[base : base + 256, :] = upright[:, p * LANES : (p + 1) * LANES]

    for big in range(8):
        for j in range(8):
            tiles[pl.ds((big * 8 + j) * 8, 8), :] = mom[
                big * 8 : big * 8 + 8, j * LANES : (j + 1) * LANES
            ]

    low = low_lanes((8, LANES))

    def beside(first, second):
        even = jnp.where(low, first, swap_halves(second))
        odd = jnp.where(low, swap_halves(first), second)
        return jnp.concatenate([even, odd], axis=0)

    def lifted(children, base):
        left = beside(children[0], children[1])
        right = beside(children[2], children[3])
        rows = jnp.concatenate([left, right], axis=1).astype(BF16)
        product = jnp.dot(
            rows, up_b[base * RANK : (base + 4) * RANK, :], preferred_element_type=F32
        )
        return jnp.where(low, product[:8], swap_halves(product[8:]))

    def tile_of(box):
        return tiles[pl.ds((box // 8) * 64 + box % 8, 8, stride=8), :]

    level_1 = [lifted([tile_of(4 * p + c) for c in range(4)], 4 * p) for p in range(16)]
    level_2 = [lifted(level_1[4 * p : 4 * p + 4], 64 + 4 * p) for p in range(4)]
    level_3 = lifted(level_2, 80)
    alone = jnp.concatenate([level_3, swap_halves(level_3)], axis=0)[:, :RANK].astype(BF16)
    product = jnp.dot(alone, up_b[84 * RANK : 85 * RANK, :], preferred_element_type=F32)
    terms[seat] = jnp.where(low, product[:8], swap_halves(product[8:]))

    sends_t = [
        whole(terms.at[seat], row_mate(v), send_t.at[v], recv_t.at[8 - v]) for v in range(1, 8)
    ]
    for copy in sends_t:
        copy.start()

    all_sends += send_part(1)

    rows_b[...] = jnp.zeros_like(rows_b)
    for row, value in enumerate(level_1 + level_2 + [level_3]):
        rows_b[pl.ds((row // 8) * 64 + row % 8, 8, stride=8), :] = value
    natural = jnp.concatenate(
        [
            jnp.concatenate(
                [rows_b[(big * 8 + j) * 8 : (big * 8 + j) * 8 + 8, :] for j in range(8)], axis=1
            )
            for big in range(4)
        ],
        axis=0,
    ).astype(BF16)
    win_b[REACH] = jnp.dot(natural, perm[...], preferred_element_type=F32).astype(BF16)

    copies[5].wait()
    first = me - REACH
    for j in range(14):
        lines[j : j + 1, :] = s0[pl.ds(j * LANES, LANES)].reshape(1, LANES) - first * 64
    lines[14:32, :] = jnp.zeros((18, LANES), jnp.int32)
    for j in range(4):
        length = min(LANES, 448 - j * LANES)
        local = sources_1[pl.ds(j * LANES, length)].reshape(1, length) - first * 16
        lines[14 + j : 15 + j, :length] = (local >> 4) * 32 + (local & 15)
    local = sources_2[...].reshape(1, 112) - first * 4
    lines[18:19, :112] = (local >> 2) * 32 + 16 + (local & 3)
    lines[19:20, :28] = (sources_3[...].reshape(1, 28) - first) * 32 + 20
    columns = lines[...].T
    places = [j * LANES for j in range(18)] + [2240, 2352]
    for j, row in enumerate(places):
        index[row : row + LANES, :] = jnp.broadcast_to(columns[:, j : j + 1], (LANES, LANES))

    slot = lax.broadcasted_iota(jnp.int32, (SUPER, LANES), 0)

    def drop_invalid(base, counts):
        limit = counts[3] + 3 * LIST
        for b in (2, 1, 0):
            limit = jnp.where(slot < (b + 1) * LIST, counts[b] + b * LIST, limit)
        rows = pl.ds(base, SUPER)
        index[rows, :] = jnp.where(slot < limit, index[rows, :], -1)

    def drop_level(first_row, counts_ref, n):
        def step(n, carry):
            base = pl.multiple_of(first_row + n * SUPER, 16)
            drop_invalid(base, [counts_ref[4 * n + b] for b in range(4)])
            return carry

        lax.fori_loop(0, n, step, 0)

    drop_level(0, counts_0, 16)
    drop_level(1792, counts_1, 4)
    drop_level(2240, counts_2, 1)
    few = lax.broadcasted_iota(jnp.int32, (48, LANES), 0)
    index[2352:2400, :] = jnp.where(few < counts_3[0], index[2352:2400, :], -1)

    def one_hot(from_row, count, width):
        place_of = index[pl.ds(from_row, count), :]
        lane = lax.broadcasted_iota(jnp.int32, (count, LANES), 1)
        hot = [
            jnp.where(place_of == lane + first_lane, 1.0, 0.0).astype(BF16)[
                :, : min(LANES, width - first_lane)
            ]
            for first_lane in range(0, width, LANES)
        ]
        return jnp.concatenate(hot, axis=1) if len(hot) > 1 else hot[0]

    def mark_0(n, carry):
        row = pl.multiple_of(n * LANES, LANES)
        hot_0[pl.ds(row, LANES), :] = one_hot(row, LANES, WINDOW * 64)
        return carry

    lax.fori_loop(0, 14, mark_0, 0)

    def mark_1(n, carry):
        row = pl.multiple_of(n * 304, 16)
        hot_1[pl.ds(row, 304), :] = one_hot(pl.multiple_of(1792 + row, 16), 304, WINDOW * 32)
        return carry

    lax.fori_loop(0, 2, mark_1, 0)

    for v in range(1, 8):
        pltpu.make_async_copy(terms.at[0], terms.at[0], recv_t.at[v]).wait()
    for n in range(2):
        four = [terms[4 * n + c] for c in range(4)]
        top[y, z, n] = (four[0] + four[1]) + (four[2] + four[3])
    sends_z = [
        whole(top.at[y, z], along_z(k), send_z.at[k], recv_z.at[rows - k])
        for k in range(1, rows)
    ]
    for copy in sends_z:
        copy.start()
    slots_4[member] = jnp.zeros((8, LANES), jnp.int32)
    slots_4[member, 0:1, :7] = sources_4[...].reshape(1, 7)
    copies[7].wait()
    sends_s = [
        whole(slots_4.at[member], mate(v), send_s.at[v], recv_s.at[4 - v]) for v in (1, 2, 3)
    ]
    sends_c = [
        whole(c4.at[member], opposite, send_c.at[0], recv_c.at[0]),
        whole(c4.at[member], sibling, send_c.at[1], recv_c.at[1]),
    ]
    for copy in sends_s + sends_c:
        copy.start()


    for copies_b in (direct(win_b, send_b, recv_b), own_rows(win_b, pass_b, recv_b)):
        start(copies_b)
        all_sends += copies_b

    def turned(rows):
        stack = jnp.concatenate(
            [rows[:, i * LANES : (i + 1) * LANES] for i in range(4)], axis=0
        )
        across = stack.T
        return jnp.concatenate([across[32 * m : 32 * m + 32] for m in range(4)], axis=1)

    def stacked(rows):
        return jnp.concatenate(
            [
                rows[:, (4 * i + m) * LANES : (4 * i + m + 1) * LANES]
                for m in range(4)
                for i in range(4)
            ],
            axis=0,
        )

    def box_tile(value):
        a, b, c, d = (value[8 * n : 8 * n + 8] for n in range(4))
        return jnp.where(low, a, d) + swap_halves(jnp.where(low, b, c))

    half = BLOCK // PIECES

    def far_part(h, rows_from, couple_from, far_from, groups, boxes):
        totals = [None] * boxes
        lane_slot = lax.broadcasted_iota(jnp.int32, (32, 512), 1) % GROUP
        for g in range(groups):
            left = turned(gathered[pl.ds(rows_from + GROUP * g, GROUP), :])
            right = stacked(
                couples[pl.ds(couple_from + GROUP * g, GROUP), h * half : (h + 1) * half]
            )
            touched = [
                b
                for b in range(boxes)
                if b * LIST < GROUP * (g + 1) and (b + 1) * LIST > GROUP * g
            ]
            if len(touched) == 2:
                border = touched[1] * LIST - GROUP * g
                zero = jnp.zeros_like(left)
                left = jnp.concatenate(
                    [
                        jnp.where(lane_slot < border, left, zero),
                        jnp.where(lane_slot < border, zero, left),
                    ],
                    axis=0,
                )
            value = jnp.dot(left, right, preferred_element_type=F32)
            for n, b in enumerate(touched):
                part = value[32 * n : 32 * n + 32]
                totals[b] = part if totals[b] is None else totals[b] + part
        for b in range(boxes):
            rows = pl.ds(far_from + 8 * b, 8)
            if h == 0:
                far[rows, :] = box_tile(totals[b])
            else:
                far[rows, :] += box_tile(totals[b])

    def gather_0(h):
        sources = win_a[h].reshape(WINDOW * 64, PART)

        def step(n, carry):
            rows = pl.ds(pl.multiple_of(n * 896, 896), 896)
            gathered[rows, :] = jnp.dot(
                hot_0[rows, :], sources, preferred_element_type=F32
            ).astype(BF16)
            return carry

        lax.fori_loop(0, 2, step, 0)

    def far_0(h, first, last):
        def step(n, carry):
            row = pl.multiple_of(n * WIDE, WIDE)
            far_part(h, row, row, pl.multiple_of(n * 64, 64), 7, 8)
            return carry

        lax.fori_loop(first, last, step, 0, unroll=4)

    arrived_direct(win_a.at[0], recv_a.at[0])
    shared = shared_rows(win_a.at[0], pass_a.at[0], recv_a.at[0])
    start(shared)
    all_sends += shared
    copies[6].wait()
    pad3[...] = jnp.zeros_like(pad3)
    pad3[0:28, :] = c3[...].astype(F32)
    couples[2352:2384, :] = pad3[...].astype(BF16)
    couples[2384:2400, :] = jnp.zeros((16, BLOCK), BF16)
    arrived_passed(win_a.at[0], recv_a.at[0])
    gather_0(0)
    copies[8].wait()
    far_0(0, 0, 4)
    arrived_direct(win_a.at[1], recv_a.at[1])
    shared = shared_rows(win_a.at[1], pass_a.at[1], recv_a.at[1])
    start(shared)
    all_sends += shared
    for k in range(1, rows):
        pltpu.make_async_copy(top.at[y, z], top.at[y, z], recv_z.at[k]).wait()
    sends_y = [
        whole(top.at[y], along_y(k), send_y.at[k], recv_y.at[planes - k])
        for k in range(1, planes)
    ]
    for copy in sends_y:
        copy.start()
    far_0(0, 4, 8)

    arrived_passed(win_a.at[1], recv_a.at[1])
    gather_0(1)
    far_0(1, 0, 4)
    back = member + 1 - 2 * lax.rem(member, 2)
    pltpu.make_async_copy(c4.at[back], c4.at[back], recv_c.at[0]).wait()
    sends_c.append(whole(c4.at[back], sibling, send_c.at[2], recv_c.at[2]))
    sends_c[2].start()
    arrived_direct(win_b, recv_b)
    shared = shared_rows(win_b, pass_b, recv_b)
    start(shared)
    all_sends += shared
    far_0(1, 4, 8)

    for k in range(1, planes):
        pltpu.make_async_copy(top.at[y], top.at[y], recv_y.at[k]).wait()
    for v in (1, 2, 3):
        pltpu.make_async_copy(slots_4.at[0], slots_4.at[0], recv_s.at[v]).wait()
    for v in (1, 2):
        pltpu.make_async_copy(c4.at[0], c4.at[0], recv_c.at[v]).wait()
    pad4[...] = jnp.zeros_like(pad4)
    for n in range(4):
        pad4[7 * n : 7 * n + 7, :] = c4[n].astype(F32)
        lines[n : n + 1, :] = slots_4[n, 0:1, :]
    columns = lines[...].T
    for n in range(4):
        index[2560 + 7 * n : 2568 + 7 * n, :] = jnp.broadcast_to(columns[:8, n : n + 1], (8, LANES))
    few = lax.broadcasted_iota(jnp.int32, (32, LANES), 0)
    index[2560:2592, :] = jnp.where(few < counts_4[group], index[2560:2592, :], -1)
    tops = 2 * rows * planes
    count = max(tops, 8)
    if tops < 8:
        tiles[0:512, :] = jnp.zeros((512, LANES), F32)
    for box in range(tops):
        tiles[pl.ds((box // 8) * 64 + box % 8, 8, stride=8), :] = top[
            box // 2 // rows, box // 2 % rows, box % 2
        ]
    natural = jnp.concatenate(
        [
            jnp.concatenate(
                [tiles[(big * 8 + j) * 8 : (big * 8 + j) * 8 + 8, :] for j in range(8)], axis=1
            )
            for big in range(count // 8)
        ],
        axis=0,
    ).astype(BF16)
    top_rows = jnp.dot(natural, perm[...], preferred_element_type=F32).astype(BF16)
    rows_4 = jnp.dot(one_hot(2560, 32, count), top_rows, preferred_element_type=F32).astype(BF16)
    blocks_4 = pad4[...].astype(BF16)
    far_4 = box_tile(
        sum(
            jnp.dot(
                turned(rows_4[:, h * PART : (h + 1) * PART]),
                stacked(blocks_4[:, h * half : (h + 1) * half]),
                preferred_element_type=F32,
            )
            for h in range(PIECES)
        )
    )

    arrived_passed(win_b, recv_b)
    copies[9].wait()
    copies[10].wait()
    for h in range(PIECES):
        gathered[0:608, :] = jnp.dot(
            hot_1[...],
            win_b[:, :, h * PART : (h + 1) * PART].reshape(WINDOW * 32, PART),
            preferred_element_type=F32,
        ).astype(BF16)

        def far_1(n, carry):
            row = pl.multiple_of(n * WIDE, WIDE)
            far_part(h, row, 1792 + row, 512 + pl.multiple_of(n * 64, 64), 7, 8)
            return carry

        lax.fori_loop(0, 2, far_1, 0)
        far_part(h, 448, 2240, 640, 5, 5)

    def lowered(parent, n, boxes):
        rows = jnp.concatenate(
            [jnp.where(low, parent, 0.0), jnp.where(low, swap_halves(parent), 0.0)], axis=0
        ).astype(BF16)
        product = lax.dot_general(
            rows,
            up_b[n * 256 : n * 256 + boxes * RANK, :],
            (((1,), (1,)), ((), ())),
            preferred_element_type=F32,
        )
        result = []
        for pair in range(0, boxes, 2):
            even = product[:8, pair * RANK : pair * RANK + LANES]
            odd = product[8:, pair * RANK : pair * RANK + LANES]
            result.append(jnp.where(low, even, swap_halves(odd)))
            result.append(jnp.where(low, swap_halves(even), odd))
        return result

    field_3 = far[672:680, :] + lowered(far_4, 21, 2)[0]
    down = lowered(field_3, 20, 4)
    field_2 = [far[640 + 8 * c : 648 + 8 * c, :] + down[c] for c in range(4)]
    field_1 = []
    for p in range(4):
        down = lowered(field_2[p], 16 + p, 4)
        for c in range(4):
            row = 512 + 8 * (4 * p + c)
            field_1.append(far[row : row + 8, :] + down[c])
    for p in range(16):
        down = lowered(field_1[p], p, 4)
        for c in range(4):
            box = 4 * p + c
            tiles[pl.ds((box // 8) * 64 + box % 8, 8, stride=8), :] = (
                far[8 * box : 8 * box + 8, :] + down[c]
            )
    for big in range(8):
        for j in range(8):
            row = (big * 8 + j) * 8
            out[big * 8 : big * 8 + 8, j * LANES : (j + 1) * LANES] = tiles[row : row + 8, :]

    for copy in sends_t + sends_s + sends_c + sends_z + sends_y:
        copy.wait_send()
    sent(all_sends)


def solution(mesh):
    devices = mesh.shape["wide"] * mesh.shape["narrow"]
    planes = max(1, devices // 32)
    split = P(("wide", "narrow"), None)
    line = P(("wide", "narrow"))
    anywhere = pl.BlockSpec(memory_space=pl.ANY)
    scalars = pl.BlockSpec(memory_space=pltpu.SMEM)
    inside = pl.BlockSpec(memory_space=pltpu.VMEM)
    vmem = pltpu.VMEM
    dma = pltpu.SemaphoreType.DMA

    def body(*arrays):
        return pl.pallas_call(
            functools.partial(kernel, devices, planes),
            out_shape=jax.ShapeDtypeStruct((64, WIDTH), F32),
            in_specs=[anywhere] * 11 + [inside] * 4 + [scalars] * 5,
            out_specs=pl.BlockSpec(memory_space=pltpu.VMEM),
            scratch_shapes=[
                vmem((64, WIDTH), F32),
                vmem((64, BLOCK), BF16),
                vmem((16, BLOCK), BF16),
                vmem((4, BLOCK), BF16),
                vmem((1, BLOCK), BF16),
                vmem((2400, BLOCK), BF16),
                vmem((28, BLOCK), BF16),
                vmem((4, 7, BLOCK), BF16),
                vmem((1792,), jnp.int32),
                vmem((32, BLOCK), F32),
                vmem((32, BLOCK), F32),
                vmem((512, LANES), F32),
                vmem((256, LANES), F32),
                vmem((WIDTH, WIDTH), BF16),
                vmem((PIECES, WINDOW, 64, PART), BF16),
                vmem((WINDOW, 32, WIDTH), BF16),
                vmem((16, BLOCK), F32),
                vmem((512, 512), BF16),
                vmem((256, 256), BF16),
                vmem((96 * RANK, LANES), BF16),
                vmem((32, LANES), jnp.int32),
                vmem((21 * LANES, LANES), jnp.int32),
                vmem((1792, WINDOW * 64), BF16),
                vmem((608, WINDOW * 32), BF16),
                vmem((1792, PART), BF16),
                vmem((85 * 8, LANES), F32),
                vmem((8, 8, LANES), F32),
                vmem((planes, devices // 8 // planes, 2, 8, LANES), F32),
                vmem((4, 8, LANES), jnp.int32),
                dma((11,)),
                dma((PIECES, 2 * REACH)),
                dma((PIECES, WINDOW)),
                dma((PIECES, WINDOW)),
                dma((2 * REACH,)),
                dma((WINDOW,)),
                dma((WINDOW,)),
                dma((8,)),
                dma((8,)),
                dma((4,)),
                dma((4,)),
                dma((4,)),
                dma((4,)),
                dma((4,)),
                dma((4,)),
                dma((3,)),
                dma((3,)),
            ],
            compiler_params=pltpu.CompilerParams(
                collective_id=0, has_side_effects=True, vmem_limit_bytes=56 * 1024 * 1024
            ),
        )(*arrays)

    return jax.shard_map(
        body,
        mesh=mesh,
        in_specs=(split,) * 10 + (line,) * 9 + (P(),),
        out_specs=split,
        check_vma=False,
    )
```
